32 devices in a mesh: snap: 4 (over y, x), space: 8 (over z, core).
Axes of the slice: x: 2, y: 2, z: 4, core: 2. Of those that a mesh axis runs over, the one named last changes fastest.
Arguments:
- field_in: bfloat16 [4, 8, 32, 32, 256], P('snap', 'space'), may hold values from -6 to 6
- ocean_mask: int32 [8, 32, 32], P('space'), may hold values 0 or 1
- cotangent: bfloat16 [4, 8, 32, 32, 256], P('snap', 'space'), may hold values from -6 to 6
- w_first: bfloat16 [3, 3, 256, 128], replicated, may hold values from -0.125 to 0.125
- b_first: float32 [128], replicated, may hold values from -3 to 3
- w_second: bfloat16 [3, 3, 128, 256], replicated, may hold values from -0.1875 to 0.1875
- b_second: float32 [256], replicated, may hold values from -3 to 3
Outputs:
- field_out: bfloat16 [4, 8, 32, 32, 256], P('snap', 'space')
- grad_field: bfloat16 [4, 8, 32, 32, 256], P('snap', 'space')
- grad_w_first: float32 [3, 3, 256, 128], P(None, None, 'space')
- grad_w_second: float32 [3, 3, 128, 256], P(None, None, 'space')
- grad_b_first: float32 [128], P('space')
- grad_b_second: float32 [256], P('space')
The draws below stay inside these ranges and needn't reach their ends.
All inputs are finite; a program needn't handle non-finite values. No bound on the sum of `ocean_mask` on one device may be relied on, other than what follows from the above.
Results may differ from the reference program's by a relative error of at most 0.014.
Values may be sent and summed in bfloat16 or wider, within the bound.
A program may use at most 64 MiB of HBM per device.

```python
import math
import jax
import jax.numpy as jnp
from jax import lax

C = 256
H = 128
DEV_COLS = 4
CY = 32
CX = 32
SNAPS = 4
REGIONS = 8
DEV_ROWS = 2
NY = 64
NX = 128


def plant(drawn, stream_key, least, top_value):
    spot = [jax.random.randint(jax.random.fold_in(stream_key, axis), (), 0, length) for axis, length in enumerate(drawn.shape)]
    longest = drawn.shape.index(max(drawn.shape))
    beside = spot[:longest] + [(spot[longest] + 1) % drawn.shape[longest]] + spot[longest + 1:]
    return drawn.at[tuple(spot)].set(least).at[tuple(beside)].set(top_value)


def block_scale(key, extent, cuts, low, high):
    gain = 1.0
    for dim, parts in cuts:
        draws = jax.random.uniform(jax.random.fold_in(jax.random.fold_in(key, 6), dim), (parts,), jnp.float32, low / len(cuts), high / len(cuts))
        gain = gain * jnp.repeat(jnp.exp(draws), extent[dim] // parts).reshape((-1,) + (1,) * (len(extent) - 1 - dim))
    return gain


def normal_values(key, extent, spread, bound, split=(), kind=jnp.bfloat16):
    level = block_scale(key, extent, split, -0.22, 0.18) if split else 1.0
    drawn = jax.random.normal(key, extent, jnp.float32) * spread * level
    return jnp.minimum(jnp.maximum(drawn, -bound), bound).astype(kind)


def setup_inputs(seed: int = 0) -> dict:
    keys = jax.random.split(jax.random.key(seed), 8)
    return {
        "field_in": normal_values(keys[0], (SNAPS, REGIONS, CY, CX, C), 1.0, 6.0, ((0, 4), (1, 8))),
        "ocean_mask": plant((jax.random.randint(keys[1], (REGIONS, CY, CX), 0, 4) < 3).astype(jnp.int32), jax.random.fold_in(keys[1], 1), 0, 1),
        "cotangent": normal_values(keys[2], (SNAPS, REGIONS, CY, CX, C), 1.0, 6.0, ((0, 4), (1, 8))),
        "w_first": normal_values(keys[3], (3, 3, C, H), (9 * C) ** -0.5, 0.125),
        "b_first": normal_values(keys[4], (H,), 0.5, 3.0, (), jnp.float32),
        "w_second": normal_values(keys[5], (3, 3, H, C), (9 * H) ** -0.5, 0.1875),
        "b_second": normal_values(keys[6], (C,), 0.5, 3.0, (), jnp.float32),
    }


ROOT_HALF = 0.7071067811865476
INV_ROOT_TWO_PI = 0.3989422804014327

def gelu_value(pre):
    return 0.5 * pre * (1.0 + lax.erf(pre * ROOT_HALF))

def gelu_slope(pre):
    return 0.5 * (1.0 + lax.erf(pre * ROOT_HALF)) + pre * jnp.exp(-0.5 * pre * pre) * INV_ROOT_TWO_PI

def to_grid(blocks):
    placed = jnp.roll(blocks, 1, axis=0)
    trailing = placed.shape[3:]
    shaped = placed.reshape((DEV_ROWS, DEV_COLS, CY, CX) + trailing)
    shaped = jnp.swapaxes(shaped, 1, 2)
    return shaped.reshape((DEV_ROWS * CY, DEV_COLS * CX) + trailing)

def to_blocks(grid):
    trailing = grid.shape[2:]
    shaped = grid.reshape((DEV_ROWS, CY, DEV_COLS, CX) + trailing)
    shaped = jnp.swapaxes(shaped, 1, 2)
    placed = shaped.reshape((REGIONS, CY, CX) + trailing)
    return jnp.roll(placed, -1, axis=0)

def dilated(source, kernel):
    return lax.conv_general_dilated(source.astype(jnp.float32)[None], kernel.astype(jnp.float32), (1, 1), ((2, 2), (2, 2)), rhs_dilation=(2, 2), dimension_numbers=('NHWC', 'HWIO', 'NHWC'), precision=lax.Precision.HIGHEST)[0]

def flipped(kernel):
    return jnp.swapaxes(kernel[::-1, ::-1], 2, 3)

def tap_sums(source, grad_out):
    padded = jnp.pad(source, ((2, 2), (2, 2), (0, 0)))
    span_y = grad_out.shape[0]
    span_x = grad_out.shape[1]
    flat_out = grad_out.reshape(span_y * span_x, grad_out.shape[2])
    tap_rows = []
    for tap_y in range(3):
        tap_line = []
        for tap_x in range(3):
            window = padded[2 * tap_y:2 * tap_y + span_y, 2 * tap_x:2 * tap_x + span_x].reshape(span_y * span_x, source.shape[2])
            tap_line.append(lax.dot_general(window, flat_out, (((0,), (0,)), ((), ())), preferred_element_type=jnp.float32))
        tap_rows.append(jnp.stack(tap_line))
    return jnp.stack(tap_rows)

def reference(field_in, ocean_mask, cotangent, w_first, b_first, w_second, b_second):
    ocean = to_grid(ocean_mask).astype(jnp.float32)[:, :, None]
    scale = 1.0 / math.sqrt(float(SNAPS * NY * NX))
    grad_wa = jnp.zeros((3, 3, C, H), jnp.float32)
    grad_wb = jnp.zeros((3, 3, H, C), jnp.float32)
    grad_ba = jnp.zeros((H,), jnp.float32)
    grad_bb = jnp.zeros((C,), jnp.float32)
    results = []
    gradients = []
    for snap_index in range(SNAPS):
        source = to_grid(field_in[snap_index])
        pre = dilated(source, w_first) + b_first
        hidden = (ocean * gelu_value(pre)).astype(jnp.bfloat16)
        mixed = dilated(hidden, w_second) + b_second
        results.append(to_blocks((source.astype(jnp.float32) + ocean * mixed).astype(jnp.bfloat16)))
        upstream = to_grid(cotangent[snap_index])
        g_mixed = (ocean * upstream.astype(jnp.float32)).astype(jnp.bfloat16)
        g_hidden = dilated(g_mixed, flipped(w_second))
        g_pre = (ocean * g_hidden * gelu_slope(pre)).astype(jnp.bfloat16)
        g_input = (upstream.astype(jnp.float32) + dilated(g_pre, flipped(w_first))).astype(jnp.bfloat16)
        gradients.append(to_blocks(g_input))
        grad_wb = grad_wb + tap_sums(hidden, g_mixed)
        grad_wa = grad_wa + tap_sums(source, g_pre)
        grad_ba = grad_ba + lax.optimization_barrier(jnp.sum(g_pre.astype(jnp.float32), axis=(0, 1)))
        grad_bb = grad_bb + lax.optimization_barrier(jnp.sum(g_mixed.astype(jnp.float32), axis=(0, 1)))
    return (jnp.stack(results), jnp.stack(gradients), grad_wa * scale, grad_wb * scale, grad_ba * scale, grad_bb * scale)
```

```python
import functools
import math

import jax
import jax.numpy as jnp
from jax import lax
from jax.experimental import pallas as pl
from jax.experimental.pallas import tpu as pltpu
from jax.sharding import PartitionSpec as P

DEV_COLS = 4
ROOT_HALF = 0.7071067811865476
INV_ROOT_TWO_PI = 0.3989422804014327
MESH = pl.DeviceIdType.MESH
F32 = jnp.float32
BF16 = jnp.bfloat16

DIRS = ((-1, 0), (1, 0), (0, -1), (0, 1), (-1, -1), (-1, 1), (1, -1), (1, 1))
UP, DOWN, LEFT, RIGHT, UP_LEFT, UP_RIGHT, DOWN_LEFT, DOWN_RIGHT = range(8)
OPPOSITE = (DOWN, UP, RIGHT, LEFT, DOWN_RIGHT, DOWN_LEFT, UP_RIGHT, UP_LEFT)

WIDE = 32
TALL = 32
CELLS = TALL * WIDE
BAND = 2 * WIDE
BLOCK = 8 * WIDE
BLOCKS = CELLS // BLOCK
EDGE = 2 * TALL
PART = 16


def mm(a, b, dims=(((1,), (0,)), ((), ()))):
    return lax.dot_general(a, b, dims, preferred_element_type=F32)


NT = (((1,), (1,)), ((), ()))
TN = (((0,), (0,)), ((), ()))


def grid2(rows, columns):
    return (
        lax.broadcasted_iota(jnp.int32, (rows, columns), 0),
        lax.broadcasted_iota(jnp.int32, (rows, columns), 1),
    )


def onehot(condition):
    return jnp.where(condition, 1.0, 0.0).astype(BF16)


def shift_left_source(rows):
    r, c = grid2(rows, rows)
    return onehot((c == r - 2) & ((r & (WIDE - 1)) >= 2))


def shift_right_source(rows):
    r, c = grid2(rows, rows)
    return onehot((c == r + 2) & ((r & (WIDE - 1)) < WIDE - 2))


def left_insert(rows, first):
    r, h = grid2(rows, PART)
    x = r & (WIDE - 1)
    return onehot((x < 2) & (h == first + 2 * (r >> 5) + x))


def right_insert(rows, first):
    r, h = grid2(rows, PART)
    x = r & (WIDE - 1)
    return onehot((x >= WIDE - 2) & (h == first + 2 * (r >> 5) + x - (WIDE - 2)))


def left_pack():
    h, r = grid2(PART, BLOCK)
    x = r & (WIDE - 1)
    return onehot((x < 2) & (h == 2 * (r >> 5) + x))


def right_pack():
    h, r = grid2(PART, BLOCK)
    x = r & (WIDE - 1)
    return onehot((x >= WIDE - 2) & (h == 2 * (r >> 5) + x - (WIDE - 2)))


def rows_of(index, size, offset=0):
    return pl.ds(pl.multiple_of(index * size + offset, 16), size)


class Halo:
    def __init__(self, geometry, own, packs, bands, corners, send_sem, recv_sem):
        self.exists, self.peer = geometry
        self.own, self.packs, self.bands, self.corners = own, packs, bands, corners
        sources = (
            own.at[pl.ds(0, BAND)],
            own.at[pl.ds(CELLS - BAND, BAND)],
            packs.at[0],
            packs.at[1],
            packs.at[0, pl.ds(0, PART)],
            packs.at[1, pl.ds(0, PART)],
            packs.at[0, pl.ds(EDGE - PART, PART)],
            packs.at[1, pl.ds(EDGE - PART, PART)],
        )
        self.copies = []
        for d in range(8):
            slot = OPPOSITE[d]
            self.copies.append(
                pltpu.make_async_remote_copy(
                    src_ref=sources[d],
                    dst_ref=self.slot(slot),
                    send_sem=send_sem.at[d],
                    recv_sem=recv_sem.at[slot],
                    device_id={"space": self.peer[d]},
                    device_id_type=MESH,
                )
            )

    def slot(self, slot):
        return self.bands.at[slot] if slot < 4 else self.corners.at[slot - 4]

    def clear_missing(self):
        for d in range(8):
            ref = self.slot(d)

            @pl.when(jnp.logical_not(self.exists[d]))
            def _():
                ref[...] = jnp.zeros(ref.shape, ref.dtype)

    def pack(self):
        to_left, to_right = left_pack(), right_pack()
        for i in range(BLOCKS):
            cells = self.own[pl.ds(i * BLOCK, BLOCK), :]
            self.packs[0, pl.ds(i * PART, PART), :] = mm(to_left, cells).astype(BF16)
            self.packs[1, pl.ds(i * PART, PART), :] = mm(to_right, cells).astype(BF16)

    def start(self):
        for d in range(8):

            @pl.when(self.exists[d])
            def _():
                self.copies[d].start()

    def wait_recv(self):
        for d in range(8):

            @pl.when(self.exists[OPPOSITE[d]])
            def _():
                self.copies[d].wait_recv()

    def wait_send(self):
        for d in range(8):

            @pl.when(self.exists[d])
            def _():
                self.copies[d].wait_send()

    def interior(self, outs, width):
        from_left, from_right = shift_left_source(BLOCK), shift_right_source(BLOCK)

        def body(i, carry):
            cells = self.own[rows_of(i, BLOCK), :]
            there = rows_of(i, BLOCK, BAND)
            shifted = (
                mm(from_left, cells).astype(BF16),
                cells,
                mm(from_right, cells).astype(BF16),
            )
            for b in range(3):
                for n, out in enumerate(outs):
                    out[there, pl.ds(b * width, width)] = shifted[b][
                        :, n * width : (n + 1) * width
                    ]
            return carry

        lax.fori_loop(0, BLOCKS, body, 0)

    def borders(self, outs, width):
        into_left, into_right = left_insert(BLOCK, 0), right_insert(BLOCK, 0)

        def body(i, carry):
            there = rows_of(i, BLOCK, BAND)
            left = mm(into_left, self.bands[LEFT, rows_of(i, PART), :]).astype(BF16)
            right = mm(into_right, self.bands[RIGHT, rows_of(i, PART), :]).astype(BF16)
            for n, out in enumerate(outs):
                mine = slice(n * width, (n + 1) * width)
                out[there, pl.ds(0, width)] = out[there, pl.ds(0, width)] + left[:, mine]
                out[there, pl.ds(2 * width, width)] = (
                    out[there, pl.ds(2 * width, width)] + right[:, mine]
                )
            return carry

        lax.fori_loop(0, BLOCKS, body, 0)
        from_left, from_right = shift_left_source(BAND), shift_right_source(BAND)
        for band, first, where, side in (
            (UP, PART - 4, 0, (UP_LEFT, UP_RIGHT)),
            (DOWN, 0, CELLS + BAND, (DOWN_LEFT, DOWN_RIGHT)),
        ):
            cells = self.bands[band]
            shifted = (
                (
                    mm(from_left, cells)
                    + mm(left_insert(BAND, first), self.corners[side[0] - 4])
                ).astype(BF16),
                cells,
                (
                    mm(from_right, cells)
                    + mm(right_insert(BAND, first), self.corners[side[1] - 4])
                ).astype(BF16),
            )
            for b in range(3):
                for n, out in enumerate(outs):
                    out[pl.ds(where, BAND), pl.ds(b * width, width)] = shifted[b][
                        :, n * width : (n + 1) * width
                    ]


class Reduction:
    def __init__(self, n_space, n_snap, share, a_in, q, b_in, t, c_in, u, d_in, sems):
        self.n_chip, self.n_snap = n_space // 2, n_snap
        self.share, self.a_in, self.q, self.b_in = share, a_in, q, b_in
        self.t, self.c_in, self.u, self.d_in = t, c_in, u, d_in
        me = lax.axis_index("space")
        snap = lax.axis_index("snap")
        self.core = lax.rem(me, 2)
        self.chip = lax.div(me, 2)
        self.snap = snap
        a_s, a_r, b_s, b_r, c_s, c_r, d_s, d_r = sems

        def copy(src, dst, send, recv, device):
            return pltpu.make_async_remote_copy(
                src_ref=src,
                dst_ref=dst,
                send_sem=send,
                recv_sem=recv,
                device_id=device,
                device_id_type=MESH,
            )

        self.a = [copy(share.at[1 - self.core], a_in, a_s, a_r, {"space": me + 1 - 2 * self.core})]
        self.b, self.c, self.d = [], [], []
        for j in range(1, n_snap):
            other = lax.rem(snap + j, n_snap)
            self.b.append(
                copy(q.at[other], b_in.at[j - 1], b_s.at[j - 1], b_r.at[j - 1], {"snap": other})
            )
            self.d.append(
                copy(u, d_in.at[j - 1], d_s.at[j - 1], d_r.at[j - 1], {"snap": other})
            )
        for j in range(1, self.n_chip):
            other = lax.rem(self.chip + j, self.n_chip)
            self.c.append(
                copy(
                    t.at[other],
                    c_in.at[j - 1],
                    c_s.at[j - 1],
                    c_r.at[j - 1],
                    {"space": 2 * other + self.core},
                )
            )

    def start_a(self):
        self.a[0].start()

    def start_b(self):
        self.a[0].wait_recv()
        for z in range(self.n_chip):
            for k in range(self.n_snap):
                both = self.share[self.core, z, k].astype(F32) + self.a_in[z, k].astype(F32)
                self.q[k, z] = both.astype(BF16)
        for c in self.b:
            c.start()

    def start_c(self):
        for c in self.b:
            c.wait_recv()
        for z in range(self.n_chip):
            total = self.q[self.snap, z].astype(F32)
            for j in range(self.n_snap - 1):
                total += self.b_in[j, z].astype(F32)
            self.t[z] = total.astype(BF16)
        for c in self.c:
            c.start()

    def start_d(self):
        for c in self.c:
            c.wait_recv()
        total = self.t[self.chip].astype(F32)
        for j in range(self.n_chip - 1):
            total += self.c_in[j].astype(F32)
        self.u[...] = total.astype(BF16)
        for c in self.d:
            c.start()

    def finish(self, scale, whole):
        for c in self.d:
            c.wait_recv()
        whole[self.snap] = self.u[...].astype(F32) * scale
        for j in range(1, self.n_snap):
            sender = lax.rem(self.snap + self.n_snap - j, self.n_snap)
            whole[sender] = self.d_in[j - 1].astype(F32) * scale

    def wait_send(self):
        for c in self.a + self.b + self.c + self.d:
            c.wait_send()


def kernel(n_space, n_snap, fused, scale, *refs):
    refs = list(refs)

    def take(count):
        got = refs[:count]
        del refs[:count]
        return got

    field, mask, cot, w1, b1, w2, b2 = take(7)
    field_out, grad_field, gw1, gw2, gb1, gb2 = take(6)
    fg, fg_packs, fg_bands, fg_corners, f3, g3, fg_send, fg_recv = take(8)
    hp, hp_packs, hp_bands, hp_corners, h3, p3, hp_send, hp_recv = take(8)
    mfull, hall, pall = take(3)
    channels, hidden_channels = field.shape[1], hp.shape[1] // 2

    me = lax.axis_index("space")
    position = lax.rem(me + 1, n_space)
    line, column = lax.div(position, DEV_COLS), lax.rem(position, DEV_COLS)
    lines = n_space // DEV_COLS
    exists, peer = [], []
    for dy, dx in DIRS:
        there = None
        if dy:
            there = (line > 0) if dy < 0 else (line < lines - 1)
        if dx:
            inside = (column > 0) if dx < 0 else (column < DEV_COLS - 1)
            there = inside if there is None else jnp.logical_and(there, inside)
        exists.append(there)
        peer.append(lax.rem(position + DEV_COLS * dy + dx - 1 + 2 * n_space, n_space))
    geometry = (exists, peer)

    reductions = []
    if fused:
        for _ in range(2):
            share, a_in, q, b_in, t, c_in, u, d_in = take(8)
            sems = take(8)
            reductions.append(
                Reduction(n_space, n_snap, share, a_in, q, b_in, t, c_in, u, d_in, sems)
            )
        (whole,) = take(1)

    first = Halo(geometry, fg, fg_packs, fg_bands, fg_corners, fg_send, fg_recv)
    second = Halo(geometry, hp, hp_packs, hp_bands, hp_corners, hp_send, hp_recv)
    first.clear_missing()
    second.clear_missing()

    barrier = pltpu.get_barrier_semaphore()
    expected = jnp.int32(0)
    for d in range(8):

        @pl.when(exists[d])
        def _():
            pl.semaphore_signal(barrier, inc=1, device_id={"space": peer[d]}, device_id_type=MESH)

        expected = expected + exists[d].astype(jnp.int32)
    if fused:
        core = lax.rem(me, 2)
        pl.semaphore_signal(
            barrier, inc=1, device_id={"space": me + 1 - 2 * core}, device_id_type=MESH
        )
        for j in range(1, n_snap):
            other = lax.rem(lax.axis_index("snap") + j, n_snap)
            pl.semaphore_signal(barrier, inc=1, device_id={"snap": other}, device_id_type=MESH)
        for j in range(1, n_space // 2):
            other = lax.rem(lax.div(me, 2) + j, n_space // 2)
            pl.semaphore_signal(
                barrier, inc=1, device_id={"space": 2 * other + core}, device_id_type=MESH
            )
        expected = expected + (1 + n_snap - 1 + n_space // 2 - 1)

    mask_bits = mask[...].astype(F32).astype(BF16)

    def prepare(i, carry):
        here = rows_of(i, BLOCK)
        r, y = grid2(BLOCK, TALL)
        lines_of = mm(onehot((r >> 5) + i * (BLOCK // WIDE) == y), mask_bits)
        r, x = grid2(BLOCK, WIDE)
        one = jnp.where((r & (WIDE - 1)) == x, lines_of, 0.0).astype(BF16)
        m = mm(one, jnp.ones((WIDE, 128), BF16))
        mfull[here, :] = m
        fg[here, pl.ds(0, channels)] = field[here, :]
        for half in range(channels // 128):
            lanes = pl.ds(half * 128, 128)
            fg[here, pl.ds(channels + half * 128, 128)] = (
                cot[here, lanes].astype(F32) * m
            ).astype(BF16)
        return carry

    lax.fori_loop(0, BLOCKS, prepare, 0)
    first.pack()
    pl.semaphore_wait(barrier, expected)
    first.start()
    first.interior((f3, g3), channels)
    pad = jnp.zeros((BAND, hidden_channels), BF16)
    for buf in (hall, pall):
        for a in range(3):
            for b in range(3):
                if a != b:
                    where = BAND * b if b < a else CELLS + BAND * (b - 1)
                    buf[pl.ds(where, BAND), pl.ds(a * hidden_channels, hidden_channels)] = pad
    first.wait_recv()
    first.borders((f3, g3), channels)

    def hidden_part(i, carry):
        here = rows_of(i, BLOCK)
        pre = jnp.zeros((BLOCK, hidden_channels), F32)
        g_hidden = jnp.zeros((BLOCK, hidden_channels), F32)
        for a in range(3):
            window = rows_of(i, BLOCK, BAND * a)
            pre += mm(f3[window, :], w1[a])
            for b in range(3):
                g_hidden += mm(
                    g3[window, pl.ds(b * channels, channels)],
                    w2[2 - a, pl.ds((2 - b) * hidden_channels, hidden_channels), :],
                    NT,
                )
        pre = pre + b1[...]
        m = mfull[here, :]
        bell = 0.5 * (1.0 + lax.erf(pre * ROOT_HALF))
        hidden = (m * (pre * bell)).astype(BF16)
        slope = bell + pre * jnp.exp(-0.5 * pre * pre) * INV_ROOT_TWO_PI
        g_pre = (m * g_hidden * slope).astype(BF16)
        hp[here, pl.ds(0, hidden_channels)] = hidden
        hp[here, pl.ds(hidden_channels, hidden_channels)] = g_pre
        for a in range(3):
            there = rows_of(i, BLOCK, BAND * a)
            lanes = pl.ds(a * hidden_channels, hidden_channels)
            hall[there, lanes] = hidden
            pall[there, lanes] = g_pre
        return carry

    lax.fori_loop(0, BLOCKS, hidden_part, 0)
    second.pack()
    second.start()

    ones = jnp.ones((PART, CELLS), BF16)
    sum_pre = mm(ones, hp[:, pl.ds(hidden_channels, hidden_channels)])
    sum_mixed = mm(ones, fg[:, pl.ds(channels, channels)])
    if fused:
        shard_c, shard_h = channels // n_space, hidden_channels // n_space
        share0, share1 = reductions[0].share, reductions[1].share
        quarter = share0.shape[3]

        def put(share, s, row, value):
            done = 0
            count = value.shape[0]
            while done < count:
                at = row + done
                k, within = at // quarter, at % quarter
                size = min(count - done, quarter - within)
                share[s % 2, s // 2, k, pl.ds(within, size), :] = value[done : done + size]
                done += size

        halves = channels // 128
        rows2 = 9 * shard_h * halves
        for b in range(3):
            sums = mm(hall[...], g3[:, pl.ds((2 - b) * channels, channels)], TN).astype(BF16)
            for a in range(3):
                part = sums[(2 - a) * hidden_channels : (3 - a) * hidden_channels]
                t = 3 * a + b
                for s in range(n_space):
                    for half in range(halves):
                        put(
                            share0,
                            s,
                            (t * halves + half) * shard_h,
                            part[s * shard_h : (s + 1) * shard_h, half * 128 : half * 128 + 128],
                        )
        r, _ = grid2(PART, 128)
        biases = jnp.where(
            r == 0,
            sum_pre,
            jnp.where(r == 1, sum_mixed[:, :128], jnp.where(r == 2, sum_mixed[:, 128:], 0.0)),
        ).astype(BF16)
        for s in range(n_space):
            put(share0, s, rows2, biases)
            left = n_snap * quarter - rows2 - PART
            if left:
                put(share0, s, rows2 + PART, jnp.zeros((left, 128), BF16))
        reductions[0].start_a()

        rows1 = 9 * shard_c
        for b in range(3):
            sums = mm(pall[...], f3[:, pl.ds(b * channels, channels)], TN)
            for a in range(3):
                part = sums[a * hidden_channels : (a + 1) * hidden_channels].T.astype(BF16)
                t = 3 * a + b
                for s in range(n_space):
                    put(share1, s, t * shard_c, part[s * shard_c : (s + 1) * shard_c])
        for s in range(n_space):
            left = n_snap * quarter - rows1
            if left:
                put(share1, s, rows1, jnp.zeros((left, 128), BF16))
        reductions[1].start_a()
        reductions[0].start_b()
    else:
        for b in range(3):
            sums = mm(hall[...], g3[:, pl.ds((2 - b) * channels, channels)], TN)
            for a in range(3):
                gw2[3 * a + b] = sums[(2 - a) * hidden_channels : (3 - a) * hidden_channels]
            sums = mm(pall[...], f3[:, pl.ds(b * channels, channels)], TN)
            for a in range(3):
                gw1[3 * a + b] = sums[a * hidden_channels : (a + 1) * hidden_channels].T
        gb1[...] = sum_pre[0:1]
        gb2[...] = sum_mixed[0:1]

    second.interior((h3, p3), hidden_channels)
    second.wait_recv()
    second.borders((h3, p3), hidden_channels)

    if fused:
        reductions[1].start_b()

    def out_part(i, carry):
        here = rows_of(i, BLOCK)
        mixed = jnp.zeros((BLOCK, channels), F32)
        for a in range(3):
            mixed += mm(h3[rows_of(i, BLOCK, BAND * a), :], w2[a])
        mixed = mixed + b2[...]
        m = mfull[here, :]
        for half in range(channels // 128):
            lanes = pl.ds(half * 128, 128)
            field_out[here, lanes] = (
                field[here, lanes].astype(F32) + m * mixed[:, half * 128 : half * 128 + 128]
            ).astype(BF16)
        return carry

    def grad_part(i, carry):
        here = rows_of(i, BLOCK)
        total = jnp.zeros((BLOCK, channels), F32)
        for a in range(3):
            window = rows_of(i, BLOCK, BAND * a)
            for b in range(3):
                total += mm(
                    p3[window, pl.ds(b * hidden_channels, hidden_channels)],
                    w1[2 - a, pl.ds((2 - b) * channels, channels), :],
                    NT,
                )
        grad_field[here, :] = (cot[here, :].astype(F32) + total).astype(BF16)
        return carry

    lax.fori_loop(0, BLOCKS, out_part, 0)
    if fused:
        reductions[0].start_c()
    lax.fori_loop(0, BLOCKS, grad_part, 0)
    if fused:
        reductions[0].start_d()
        reductions[1].start_c()
        reductions[0].finish(scale, whole)

        def get(row, count):
            pieces = []
            done = 0
            while done < count:
                at = row + done
                k, within = at // quarter, at % quarter
                size = min(count - done, quarter - within)
                pieces.append(whole[k, pl.ds(within, size), :])
                done += size
            return pieces[0] if len(pieces) == 1 else jnp.concatenate(pieces, axis=0)

        for t in range(9):
            for half in range(halves):
                gw2[t, :, pl.ds(half * 128, 128)] = get((t * halves + half) * shard_h, shard_h)
        tail = get(rows2, PART)
        r, c = grid2(128, shard_h)
        pick = jnp.where(r == c + me * shard_h, 1.0, 0.0)
        gb1[...] = jnp.dot(
            tail, pick, preferred_element_type=F32, precision=lax.Precision.HIGHEST
        )[0:1]
        picked = jnp.zeros((PART, shard_c), F32)
        for half in range(halves):
            r, c = grid2(128, shard_c)
            pick = jnp.where(r + half * 128 == c + me * shard_c, 1.0, 0.0)
            picked = picked + jnp.where(
                lax.broadcasted_iota(jnp.int32, (PART, shard_c), 0) == 1 + half,
                jnp.dot(tail, pick, preferred_element_type=F32, precision=lax.Precision.HIGHEST),
                0.0,
            )
        gb2[...] = jnp.sum(picked, axis=0, keepdims=True)

        reductions[1].start_d()
        reductions[1].finish(scale, whole)
        for t in range(9):
            gw1[t] = get(t * shard_c, shard_c)
        for red in reductions:
            red.wait_send()
    first.wait_send()
    second.wait_send()


def local(field_in, ocean_mask, cotangent, w_first, b_first, w_second, b_second):
    n_space, n_snap = lax.axis_size("space"), lax.axis_size("snap")
    tall, wide, channels = field_in.shape[2:]
    hidden_channels = w_first.shape[3]
    total = field_in.shape[0] * n_snap * n_space * tall * wide
    scale = 1.0 / math.sqrt(float(total))
    cells = tall * wide
    shard_c, shard_h = channels // n_space, hidden_channels // n_space
    fused = shard_c % 16 == 0 and shard_h % 16 == 0

    def halo_scratch(width):
        return [
            pltpu.VMEM((cells, width), BF16),
            pltpu.VMEM((2, EDGE, width), BF16),
            pltpu.VMEM((4, BAND, width), BF16),
            pltpu.VMEM((4, PART, width), BF16),
            pltpu.VMEM((cells + 2 * BAND, 3 * width // 2), BF16),
            pltpu.VMEM((cells + 2 * BAND, 3 * width // 2), BF16),
            pltpu.SemaphoreType.DMA((8,)),
            pltpu.SemaphoreType.DMA((8,)),
        ]

    scratch = halo_scratch(2 * channels) + halo_scratch(2 * hidden_channels)
    scratch += [
        pltpu.VMEM((cells, 128), F32),
        pltpu.VMEM((cells + 2 * BAND, 3 * hidden_channels), BF16),
        pltpu.VMEM((cells + 2 * BAND, 3 * hidden_channels), BF16),
    ]
    if fused:
        chips = n_space // 2
        need = max(9 * shard_c * hidden_channels // 128, 9 * shard_h * channels // 128 + PART)
        quarter = -(-need // (PART * n_snap)) * PART
        for _ in range(2):
            piece = (quarter, 128)
            scratch += [
                pltpu.VMEM((2, chips, n_snap) + piece, BF16),
                pltpu.VMEM((chips, n_snap) + piece, BF16),
                pltpu.VMEM((n_snap, chips) + piece, BF16),
                pltpu.VMEM((n_snap - 1, chips) + piece, BF16),
                pltpu.VMEM((chips,) + piece, BF16),
                pltpu.VMEM((chips - 1,) + piece, BF16),
                pltpu.VMEM(piece, BF16),
                pltpu.VMEM((n_snap - 1,) + piece, BF16),
                pltpu.SemaphoreType.DMA,
                pltpu.SemaphoreType.DMA,
                pltpu.SemaphoreType.DMA((n_snap - 1,)),
                pltpu.SemaphoreType.DMA((n_snap - 1,)),
                pltpu.SemaphoreType.DMA((chips - 1,)),
                pltpu.SemaphoreType.DMA((chips - 1,)),
                pltpu.SemaphoreType.DMA((n_snap - 1,)),
                pltpu.SemaphoreType.DMA((n_snap - 1,)),
            ]
        scratch += [pltpu.VMEM((n_snap, quarter, 128), F32)]
        grads = [
            jax.ShapeDtypeStruct((9, shard_c, hidden_channels), F32),
            jax.ShapeDtypeStruct((9, shard_h, channels), F32),
            jax.ShapeDtypeStruct((1, shard_h), F32),
            jax.ShapeDtypeStruct((1, shard_c), F32),
        ]
    else:
        grads = [
            jax.ShapeDtypeStruct((9, channels, hidden_channels), F32),
            jax.ShapeDtypeStruct((9, hidden_channels, channels), F32),
            jax.ShapeDtypeStruct((1, hidden_channels), F32),
            jax.ShapeDtypeStruct((1, channels), F32),
        ]
    vmem = pl.BlockSpec(memory_space=pltpu.VMEM)
    field_out, grad_field, gw1, gw2, gb1, gb2 = pl.pallas_call(
        functools.partial(kernel, n_space, n_snap, fused, scale),
        out_shape=[jax.ShapeDtypeStruct((cells, channels), BF16)] * 2 + grads,
        in_specs=[vmem] * 7,
        out_specs=[vmem] * 6,
        scratch_shapes=scratch,
        compiler_params=pltpu.CompilerParams(
            collective_id=0, has_side_effects=True, vmem_limit_bytes=48 * 1024 * 1024
        ),
    )(
        field_in.reshape(cells, channels),
        ocean_mask.reshape(tall, wide),
        cotangent.reshape(cells, channels),
        w_first.reshape(3, 3 * channels, hidden_channels),
        b_first.reshape(1, hidden_channels),
        w_second.reshape(3, 3 * hidden_channels, channels),
        b_second.reshape(1, channels),
    )
    whole_shape = field_in.shape
    if not fused:
        sums = (
            lax.psum_scatter(gw1, "space", scatter_dimension=1, tiled=True),
            lax.psum_scatter(gw2, "space", scatter_dimension=1, tiled=True),
            lax.psum_scatter(gb1[0], "space", scatter_dimension=0, tiled=True),
            lax.psum_scatter(gb2[0], "space", scatter_dimension=0, tiled=True),
        )
        gw1, gw2, gb1, gb2 = [value * scale for value in lax.psum(sums, "snap")]
    return (
        field_out.reshape(whole_shape),
        grad_field.reshape(whole_shape),
        gw1.reshape(3, 3, shard_c, hidden_channels),
        gw2.reshape(3, 3, shard_h, channels),
        gb1.reshape(shard_h),
        gb2.reshape(shard_c),
    )


def solution(mesh):
    placed = (
        P("snap", "space", None, None, None),
        P("space", None, None),
        P("snap", "space", None, None, None),
        P(),
        P(),
        P(),
        P(),
    )
    return jax.shard_map(
        local,
        mesh=mesh,
        in_specs=placed,
        out_specs=(
            P("snap", "space", None, None, None),
            P("snap", "space", None, None, None),
            P(None, None, "space", None),
            P(None, None, "space", None),
            P("space"),
            P("space"),
        ),
        check_vma=False,
    )
```

```python
import functools
import math

import jax
import jax.numpy as jnp
from jax import lax
from jax.experimental import pallas as pl
from jax.experimental.pallas import tpu as pltpu
from jax.sharding import PartitionSpec as P

DEV_COLS = 4
ROOT_HALF = 0.7071067811865476
INV_ROOT_TWO_PI = 0.3989422804014327
MESH = pl.DeviceIdType.MESH
F32 = jnp.float32
BF16 = jnp.bfloat16

DIRS = ((-1, 0), (1, 0), (0, -1), (0, 1), (-1, -1), (-1, 1), (1, -1), (1, 1))
UP, DOWN, LEFT, RIGHT, UP_LEFT, UP_RIGHT, DOWN_LEFT, DOWN_RIGHT = range(8)
OPPOSITE = (DOWN, UP, RIGHT, LEFT, DOWN_RIGHT, DOWN_LEFT, UP_RIGHT, UP_LEFT)

WIDE = 32
TALL = 32
CELLS = TALL * WIDE
BAND = 2 * WIDE
BLOCK = 8 * WIDE
BLOCKS = CELLS // BLOCK
STEP = CELLS // 2
EDGE = 2 * TALL
PART = 16


def mm(a, b, dims=(((1,), (0,)), ((), ()))):
    return lax.dot_general(a, b, dims, preferred_element_type=F32)


NT = (((1,), (1,)), ((), ()))
TN = (((0,), (0,)), ((), ()))


def grid2(rows, columns):
    return (
        lax.broadcasted_iota(jnp.int32, (rows, columns), 0),
        lax.broadcasted_iota(jnp.int32, (rows, columns), 1),
    )


def onehot(condition):
    return jnp.where(condition, 1.0, 0.0).astype(BF16)


def shift_left_source(rows):
    r, c = grid2(rows, rows)
    return onehot((c == r - 2) & ((r & (WIDE - 1)) >= 2))


def shift_right_source(rows):
    r, c = grid2(rows, rows)
    return onehot((c == r + 2) & ((r & (WIDE - 1)) < WIDE - 2))


def left_insert(rows, first):
    r, h = grid2(rows, PART)
    x = r & (WIDE - 1)
    return onehot((x < 2) & (h == first + 2 * (r >> 5) + x))


def right_insert(rows, first):
    r, h = grid2(rows, PART)
    x = r & (WIDE - 1)
    return onehot((x >= WIDE - 2) & (h == first + 2 * (r >> 5) + x - (WIDE - 2)))


def left_pack():
    h, r = grid2(PART, BLOCK)
    x = r & (WIDE - 1)
    return onehot((x < 2) & (h == 2 * (r >> 5) + x))


def right_pack():
    h, r = grid2(PART, BLOCK)
    x = r & (WIDE - 1)
    return onehot((x >= WIDE - 2) & (h == 2 * (r >> 5) + x - (WIDE - 2)))


def rows_of(index, size, offset=0):
    return pl.ds(pl.multiple_of(index * size + offset, 16), size)


class Halo:
    def __init__(self, geometry, own, packs, bands, corners, send_sem, recv_sem):
        self.exists, self.peer = geometry
        self.own, self.packs, self.bands, self.corners = own, packs, bands, corners
        sources = (
            own.at[pl.ds(0, BAND)],
            own.at[pl.ds(CELLS - BAND, BAND)],
            packs.at[0],
            packs.at[1],
            packs.at[0, pl.ds(0, PART)],
            packs.at[1, pl.ds(0, PART)],
            packs.at[0, pl.ds(EDGE - PART, PART)],
            packs.at[1, pl.ds(EDGE - PART, PART)],
        )
        self.copies = []
        for d in range(8):
            slot = OPPOSITE[d]
            self.copies.append(
                pltpu.make_async_remote_copy(
                    src_ref=sources[d],
                    dst_ref=self.slot(slot),
                    send_sem=send_sem.at[d],
                    recv_sem=recv_sem.at[slot],
                    device_id={"space": self.peer[d]},
                    device_id_type=MESH,
                )
            )

    def slot(self, slot):
        return self.bands.at[slot] if slot < 4 else self.corners.at[slot - 4]

    def clear_missing(self):
        for d in range(8):
            ref = self.slot(d)

            @pl.when(jnp.logical_not(self.exists[d]))
            def _():
                ref[...] = jnp.zeros(ref.shape, ref.dtype)

    def pack(self):
        to_left, to_right = left_pack(), right_pack()
        for i in range(BLOCKS):
            cells = self.own[pl.ds(i * BLOCK, BLOCK), :]
            self.packs[0, pl.ds(i * PART, PART), :] = mm(to_left, cells).astype(BF16)
            self.packs[1, pl.ds(i * PART, PART), :] = mm(to_right, cells).astype(BF16)

    def start(self):
        for d in range(8):

            @pl.when(self.exists[d])
            def _():
                self.copies[d].start()

    def wait_recv(self):
        for d in range(8):

            @pl.when(self.exists[OPPOSITE[d]])
            def _():
                self.copies[d].wait_recv()

    def wait_send(self):
        for d in range(8):

            @pl.when(self.exists[d])
            def _():
                self.copies[d].wait_send()

    def interior(self, outs, width):
        from_left, from_right = shift_left_source(BLOCK), shift_right_source(BLOCK)

        def body(i, carry):
            cells = self.own[rows_of(i, BLOCK), :]
            there = rows_of(i, BLOCK, BAND)
            shifted = (
                mm(from_left, cells).astype(BF16),
                cells,
                mm(from_right, cells).astype(BF16),
            )
            for b in range(3):
                for n, out in enumerate(outs):
                    out[there, pl.ds(b * width, width)] = shifted[b][
                        :, n * width : (n + 1) * width
                    ]
            return carry

        lax.fori_loop(0, BLOCKS, body, 0)

    def borders(self, outs, width):
        into_left, into_right = left_insert(BLOCK, 0), right_insert(BLOCK, 0)

        def body(i, carry):
            there = rows_of(i, BLOCK, BAND)
            left = mm(into_left, self.bands[LEFT, rows_of(i, PART), :]).astype(BF16)
            right = mm(into_right, self.bands[RIGHT, rows_of(i, PART), :]).astype(BF16)
            for n, out in enumerate(outs):
                mine = slice(n * width, (n + 1) * width)
                out[there, pl.ds(0, width)] = out[there, pl.ds(0, width)] + left[:, mine]
                out[there, pl.ds(2 * width, width)] = (
                    out[there, pl.ds(2 * width, width)] + right[:, mine]
                )
            return carry

        lax.fori_loop(0, BLOCKS, body, 0)
        from_left, from_right = shift_left_source(BAND), shift_right_source(BAND)
        for band, first, where, side in (
            (UP, PART - 4, 0, (UP_LEFT, UP_RIGHT)),
            (DOWN, 0, CELLS + BAND, (DOWN_LEFT, DOWN_RIGHT)),
        ):
            cells = self.bands[band]
            shifted = (
                (
                    mm(from_left, cells)
                    + mm(left_insert(BAND, first), self.corners[side[0] - 4])
                ).astype(BF16),
                cells,
                (
                    mm(from_right, cells)
                    + mm(right_insert(BAND, first), self.corners[side[1] - 4])
                ).astype(BF16),
            )
            for b in range(3):
                for n, out in enumerate(outs):
                    out[pl.ds(where, BAND), pl.ds(b * width, width)] = shifted[b][
                        :, n * width : (n + 1) * width
                    ]


class Reduction:
    def __init__(self, n_space, n_snap, share, a_in, q, b_in, t, c_in, u, d_in, sems):
        self.n_chip, self.n_snap = n_space // 2, n_snap
        self.share, self.a_in, self.q, self.b_in = share, a_in, q, b_in
        self.t, self.c_in, self.u, self.d_in = t, c_in, u, d_in
        me = lax.axis_index("space")
        snap = lax.axis_index("snap")
        self.core = lax.rem(me, 2)
        self.chip = lax.div(me, 2)
        self.snap = snap
        a_s, a_r, b_s, b_r, c_s, c_r, d_s, d_r = sems

        def copy(src, dst, send, recv, device):
            return pltpu.make_async_remote_copy(
                src_ref=src,
                dst_ref=dst,
                send_sem=send,
                recv_sem=recv,
                device_id=device,
                device_id_type=MESH,
            )

        self.a = [copy(share.at[1 - self.core], a_in, a_s, a_r, {"space": me + 1 - 2 * self.core})]
        self.b, self.c, self.d = [], [], []
        for j in range(1, n_snap):
            other = lax.rem(snap + j, n_snap)
            self.b.append(
                copy(q.at[other], b_in.at[j - 1], b_s.at[j - 1], b_r.at[j - 1], {"snap": other})
            )
            self.d.append(
                copy(u, d_in.at[j - 1], d_s.at[j - 1], d_r.at[j - 1], {"snap": other})
            )
        for j in range(1, self.n_chip):
            other = lax.rem(self.chip + j, self.n_chip)
            self.c.append(
                copy(
                    t.at[other],
                    c_in.at[j - 1],
                    c_s.at[j - 1],
                    c_r.at[j - 1],
                    {"space": 2 * other + self.core},
                )
            )

    def start_a(self):
        self.a[0].start()

    def start_b(self):
        self.a[0].wait_recv()
        for z in range(self.n_chip):
            for k in range(self.n_snap):
                both = self.share[self.core, z, k].astype(F32) + self.a_in[z, k].astype(F32)
                self.q[k, z] = both.astype(BF16)
        for c in self.b:
            c.start()

    def start_c(self):
        for c in self.b:
            c.wait_recv()
        for z in range(self.n_chip):
            total = self.q[self.snap, z].astype(F32)
            for j in range(self.n_snap - 1):
                total += self.b_in[j, z].astype(F32)
            self.t[z] = total.astype(BF16)
        for c in self.c:
            c.start()

    def start_d(self):
        for c in self.c:
            c.wait_recv()
        total = self.t[self.chip].astype(F32)
        for j in range(self.n_chip - 1):
            total += self.c_in[j].astype(F32)
        self.u[...] = total.astype(BF16)
        for c in self.d:
            c.start()

    def finish(self, scale, whole):
        for c in self.d:
            c.wait_recv()
        whole[self.snap] = self.u[...].astype(F32) * scale
        for j in range(1, self.n_snap):
            sender = lax.rem(self.snap + self.n_snap - j, self.n_snap)
            whole[sender] = self.d_in[j - 1].astype(F32) * scale

    def wait_send(self):
        for c in self.a + self.b + self.c + self.d:
            c.wait_send()


def kernel(n_space, n_snap, fused, scale, *refs):
    refs = list(refs)

    def take(count):
        got = refs[:count]
        del refs[:count]
        return got

    sources = take(7)
    field_dst, grad_dst, gw1, gw2, gb1, gb2 = take(6)
    fg, fg_packs, fg_bands, fg_corners, f3, g3, fg_send, fg_recv = take(8)
    hp, hp_packs, hp_bands, hp_corners, h3, p3, hp_send, hp_recv = take(8)
    mfull, hall, pall, w1t, w2t = take(5)
    mask, cot, w1, b1, w2, b2, load_sem = take(7)
    field_out, grad_field, store_sem = take(3)
    stores = [
        pltpu.make_async_copy(field_out, field_dst, store_sem.at[0]),
        pltpu.make_async_copy(grad_field, grad_dst, store_sem.at[1]),
    ]
    channels, hidden_channels = cot.shape[1], hp.shape[1] // 2
    field = fg.at[:, pl.ds(0, channels)]
    loads = [
        pltpu.make_async_copy(src, dst, load_sem.at[n])
        for n, (src, dst) in enumerate(zip(sources, (field, mask, cot, w1, b1, w2, b2)))
    ]
    for n in (1, 2, 0, 3, 5, 4, 6):
        loads[n].start()

    me = lax.axis_index("space")
    position = lax.rem(me + 1, n_space)
    line, column = lax.div(position, DEV_COLS), lax.rem(position, DEV_COLS)
    lines = n_space // DEV_COLS
    exists, peer = [], []
    for dy, dx in DIRS:
        there = None
        if dy:
            there = (line > 0) if dy < 0 else (line < lines - 1)
        if dx:
            inside = (column > 0) if dx < 0 else (column < DEV_COLS - 1)
            there = inside if there is None else jnp.logical_and(there, inside)
        exists.append(there)
        peer.append(lax.rem(position + DEV_COLS * dy + dx - 1 + 2 * n_space, n_space))
    geometry = (exists, peer)

    reductions = []
    if fused:
        for _ in range(2):
            share, a_in, q, b_in, t, c_in, u, d_in = take(8)
            sems = take(8)
            reductions.append(
                Reduction(n_space, n_snap, share, a_in, q, b_in, t, c_in, u, d_in, sems)
            )
        (whole,) = take(1)

    first = Halo(geometry, fg, fg_packs, fg_bands, fg_corners, fg_send, fg_recv)
    second = Halo(geometry, hp, hp_packs, hp_bands, hp_corners, hp_send, hp_recv)

    barrier = pltpu.get_barrier_semaphore()
    expected = jnp.int32(0)
    for d in range(8):

        @pl.when(exists[d])
        def _():
            pl.semaphore_signal(barrier, inc=1, device_id={"space": peer[d]}, device_id_type=MESH)

        expected = expected + exists[d].astype(jnp.int32)
    if fused:
        core = lax.rem(me, 2)
        pl.semaphore_signal(
            barrier, inc=1, device_id={"space": me + 1 - 2 * core}, device_id_type=MESH
        )
        for j in range(1, n_snap):
            other = lax.rem(lax.axis_index("snap") + j, n_snap)
            pl.semaphore_signal(barrier, inc=1, device_id={"snap": other}, device_id_type=MESH)
        for j in range(1, n_space // 2):
            other = lax.rem(lax.div(me, 2) + j, n_space // 2)
            pl.semaphore_signal(
                barrier, inc=1, device_id={"space": 2 * other + core}, device_id_type=MESH
            )
        expected = expected + (1 + n_snap - 1 + n_space // 2 - 1)

    first.clear_missing()
    second.clear_missing()
    for n in (1, 2, 0):
        loads[n].wait()

    mask_bits = mask[...].astype(F32).astype(BF16)

    def prepare(i, carry):
        here = rows_of(i, BLOCK)
        r, y = grid2(BLOCK, TALL)
        lines_of = mm(onehot((r >> 5) + i * (BLOCK // WIDE) == y), mask_bits)
        r, x = grid2(BLOCK, WIDE)
        one = jnp.where((r & (WIDE - 1)) == x, lines_of, 0.0).astype(BF16)
        m = mm(one, jnp.ones((WIDE, 128), BF16))
        mfull[here, :] = m
        for half in range(channels // 128):
            lanes = pl.ds(half * 128, 128)
            fg[here, pl.ds(channels + half * 128, 128)] = (
                cot[here, lanes].astype(F32) * m
            ).astype(BF16)
        return carry

    lax.fori_loop(0, BLOCKS, prepare, 0)
    first.pack()
    pl.semaphore_wait(barrier, expected)
    first.start()
    first.interior((f3, g3), channels)
    for n in (3, 4, 5, 6):
        loads[n].wait()
    for a in range(3):
        for b in range(3):
            w2t[a, pl.ds(b * channels, channels), :] = w2[
                2 - a, pl.ds((2 - b) * hidden_channels, hidden_channels), :
            ].T
            w1t[a, pl.ds(b * hidden_channels, hidden_channels), :] = w1[
                2 - a, pl.ds((2 - b) * channels, channels), :
            ].T
    pad = jnp.zeros((BAND, hidden_channels), BF16)
    for buf in (hall, pall):
        for a in range(3):
            for b in range(3):
                if a != b:
                    where = BAND * b if b < a else CELLS + BAND * (b - 1)
                    buf[pl.ds(where, BAND), pl.ds(a * hidden_channels, hidden_channels)] = pad
    first.wait_recv()
    first.borders((f3, g3), channels)

    def hidden_part(i, carry):
        here = rows_of(i, STEP)
        pre = jnp.zeros((STEP, hidden_channels), F32)
        g_hidden = jnp.zeros((STEP, hidden_channels), F32)
        for a in range(3):
            window = rows_of(i, STEP, BAND * a)
            pre += mm(f3[window, :], w1[a])
            g_hidden += mm(g3[window, :], w2t[a])
        pre = pre + b1[...]
        m = mfull[here, :]
        bell = 0.5 * (1.0 + lax.erf(pre * ROOT_HALF))
        hidden = (m * (pre * bell)).astype(BF16)
        slope = bell + pre * jnp.exp(-0.5 * pre * pre) * INV_ROOT_TWO_PI
        g_pre = (m * g_hidden * slope).astype(BF16)
        hp[here, pl.ds(0, hidden_channels)] = hidden
        hp[here, pl.ds(hidden_channels, hidden_channels)] = g_pre
        for a in range(3):
            there = rows_of(i, STEP, BAND * a)
            lanes = pl.ds(a * hidden_channels, hidden_channels)
            hall[there, lanes] = hidden
            pall[there, lanes] = g_pre
        return carry

    lax.fori_loop(0, CELLS // STEP, hidden_part, 0)
    second.pack()
    second.start()

    ones = jnp.ones((PART, CELLS), BF16)
    sum_pre = mm(ones, hp[:, pl.ds(hidden_channels, hidden_channels)])
    sum_mixed = mm(ones, fg[:, pl.ds(channels, channels)])
    if fused:
        shard_c, shard_h = channels // n_space, hidden_channels // n_space
        share0, share1 = reductions[0].share, reductions[1].share
        quarter = share0.shape[3]

        def put(share, s, row, value):
            done = 0
            count = value.shape[0]
            while done < count:
                at = row + done
                k, within = at // quarter, at % quarter
                size = min(count - done, quarter - within)
                share[s % 2, s // 2, k, pl.ds(within, size), :] = value[done : done + size]
                done += size

        halves = channels // 128
        rows2 = 9 * shard_h * halves
        all_sums = mm(hall[...], g3[...], TN).astype(BF16)
        for b in range(3):
            sums = all_sums[:, (2 - b) * channels : (3 - b) * channels]
            for a in range(3):
                part = sums[(2 - a) * hidden_channels : (3 - a) * hidden_channels]
                t = 3 * a + b
                for s in range(n_space):
                    for half in range(halves):
                        put(
                            share0,
                            s,
                            (t * halves + half) * shard_h,
                            part[s * shard_h : (s + 1) * shard_h, half * 128 : half * 128 + 128],
                        )
        r, _ = grid2(PART, 128)
        biases = jnp.where(
            r == 0,
            sum_pre,
            jnp.where(r == 1, sum_mixed[:, :128], jnp.where(r == 2, sum_mixed[:, 128:], 0.0)),
        ).astype(BF16)
        for s in range(n_space):
            put(share0, s, rows2, biases)
            left = n_snap * quarter - rows2 - PART
            if left:
                put(share0, s, rows2 + PART, jnp.zeros((left, 128), BF16))
        reductions[0].start_a()

        rows1 = 9 * shard_c
        all_sums = mm(pall[...], f3[...], TN)
        for b in range(3):
            sums = all_sums[:, b * channels : (b + 1) * channels]
            for a in range(3):
                part = sums[a * hidden_channels : (a + 1) * hidden_channels].T.astype(BF16)
                t = 3 * a + b
                for s in range(n_space):
                    put(share1, s, t * shard_c, part[s * shard_c : (s + 1) * shard_c])
        for s in range(n_space):
            left = n_snap * quarter - rows1
            if left:
                put(share1, s, rows1, jnp.zeros((left, 128), BF16))
        reductions[1].start_a()
        reductions[0].start_b()
    else:
        for b in range(3):
            sums = mm(hall[...], g3[:, pl.ds((2 - b) * channels, channels)], TN)
            for a in range(3):
                gw2[3 * a + b] = sums[(2 - a) * hidden_channels : (3 - a) * hidden_channels]
            sums = mm(pall[...], f3[:, pl.ds(b * channels, channels)], TN)
            for a in range(3):
                gw1[3 * a + b] = sums[a * hidden_channels : (a + 1) * hidden_channels].T
        gb1[...] = sum_pre[0:1]
        gb2[...] = sum_mixed[0:1]

    second.interior((h3, p3), hidden_channels)
    second.wait_recv()
    second.borders((h3, p3), hidden_channels)

    if fused:
        reductions[1].start_b()

    def out_part(i, carry):
        here = rows_of(i, STEP)
        mixed = jnp.zeros((STEP, channels), F32)
        for a in range(3):
            mixed += mm(h3[rows_of(i, STEP, BAND * a), :], w2[a])
        mixed = mixed + b2[...]
        m = mfull[here, :]
        for half in range(channels // 128):
            lanes = pl.ds(half * 128, 128)
            field_out[here, lanes] = (
                field[here, lanes].astype(F32) + m * mixed[:, half * 128 : half * 128 + 128]
            ).astype(BF16)
        return carry

    def grad_part(i, carry):
        here = rows_of(i, STEP)
        total = jnp.zeros((STEP, channels), F32)
        for a in range(3):
            total += mm(p3[rows_of(i, STEP, BAND * a), :], w1t[a])
        grad_field[here, :] = (cot[here, :].astype(F32) + total).astype(BF16)
        return carry

    lax.fori_loop(0, CELLS // STEP, out_part, 0)
    stores[0].start()
    if fused:
        reductions[0].start_c()
    lax.fori_loop(0, CELLS // STEP, grad_part, 0)
    stores[1].start()
    if fused:
        reductions[0].start_d()
        reductions[1].start_c()
        reductions[0].finish(scale, whole)

        def get(row, count):
            pieces = []
            done = 0
            while done < count:
                at = row + done
                k, within = at // quarter, at % quarter
                size = min(count - done, quarter - within)
                pieces.append(whole[k, pl.ds(within, size), :])
                done += size
            return pieces[0] if len(pieces) == 1 else jnp.concatenate(pieces, axis=0)

        for t in range(9):
            for half in range(halves):
                gw2[t, :, pl.ds(half * 128, 128)] = get((t * halves + half) * shard_h, shard_h)
        tail = get(rows2, PART)
        r, c = grid2(128, shard_h)
        pick = jnp.where(r == c + me * shard_h, 1.0, 0.0)
        gb1[...] = jnp.dot(
            tail, pick, preferred_element_type=F32, precision=lax.Precision.HIGHEST
        )[0:1]
        picked = jnp.zeros((PART, shard_c), F32)
        for half in range(halves):
            r, c = grid2(128, shard_c)
            pick = jnp.where(r + half * 128 == c + me * shard_c, 1.0, 0.0)
            picked = picked + jnp.where(
                lax.broadcasted_iota(jnp.int32, (PART, shard_c), 0) == 1 + half,
                jnp.dot(tail, pick, preferred_element_type=F32, precision=lax.Precision.HIGHEST),
                0.0,
            )
        gb2[...] = jnp.sum(picked, axis=0, keepdims=True)

        reductions[1].start_d()
        reductions[1].finish(scale, whole)
        for t in range(9):
            gw1[t] = get(t * shard_c, shard_c)
        for red in reductions:
            red.wait_send()
    first.wait_send()
    second.wait_send()
    for c in stores:
        c.wait()


def store_all(*refs):
    sem = refs[-1]
    copies = [
        pltpu.make_async_copy(refs[n], refs[6 + n], sem.at[n]) for n in range(6)
    ]
    for c in copies:
        c.start()
    for c in copies:
        c.wait()


def local(field_in, ocean_mask, cotangent, w_first, b_first, w_second, b_second):
    n_space, n_snap = lax.axis_size("space"), lax.axis_size("snap")
    tall, wide, channels = field_in.shape[2:]
    hidden_channels = w_first.shape[3]
    total = field_in.shape[0] * n_snap * n_space * tall * wide
    scale = 1.0 / math.sqrt(float(total))
    cells = tall * wide
    shard_c, shard_h = channels // n_space, hidden_channels // n_space
    fused = shard_c % 16 == 0 and shard_h % 16 == 0

    def halo_scratch(width):
        return [
            pltpu.VMEM((cells, width), BF16),
            pltpu.VMEM((2, EDGE, width), BF16),
            pltpu.VMEM((4, BAND, width), BF16),
            pltpu.VMEM((4, PART, width), BF16),
            pltpu.VMEM((cells + 2 * BAND, 3 * width // 2), BF16),
            pltpu.VMEM((cells + 2 * BAND, 3 * width // 2), BF16),
            pltpu.SemaphoreType.DMA((8,)),
            pltpu.SemaphoreType.DMA((8,)),
        ]

    scratch = halo_scratch(2 * channels) + halo_scratch(2 * hidden_channels)
    scratch += [
        pltpu.VMEM((cells, 128), F32),
        pltpu.VMEM((cells + 2 * BAND, 3 * hidden_channels), BF16),
        pltpu.VMEM((cells + 2 * BAND, 3 * hidden_channels), BF16),
        pltpu.VMEM((3, 3 * hidden_channels, channels), BF16),
        pltpu.VMEM((3, 3 * channels, hidden_channels), BF16),
        pltpu.VMEM((tall, wide), jnp.int32),
        pltpu.VMEM((cells, channels), BF16),
        pltpu.VMEM((3, 3 * channels, hidden_channels), BF16),
        pltpu.VMEM((1, hidden_channels), F32),
        pltpu.VMEM((3, 3 * hidden_channels, channels), BF16),
        pltpu.VMEM((1, channels), F32),
        pltpu.SemaphoreType.DMA((7,)),
        pltpu.VMEM((cells, channels), BF16),
        pltpu.VMEM((cells, channels), BF16),
        pltpu.SemaphoreType.DMA((2,)),
    ]
    if fused:
        chips = n_space // 2
        need = max(9 * shard_c * hidden_channels // 128, 9 * shard_h * channels // 128 + PART)
        quarter = -(-need // (PART * n_snap)) * PART
        for _ in range(2):
            piece = (quarter, 128)
            scratch += [
                pltpu.VMEM((2, chips, n_snap) + piece, BF16),
                pltpu.VMEM((chips, n_snap) + piece, BF16),
                pltpu.VMEM((n_snap, chips) + piece, BF16),
                pltpu.VMEM((n_snap - 1, chips) + piece, BF16),
                pltpu.VMEM((chips,) + piece, BF16),
                pltpu.VMEM((chips - 1,) + piece, BF16),
                pltpu.VMEM(piece, BF16),
                pltpu.VMEM((n_snap - 1,) + piece, BF16),
                pltpu.SemaphoreType.DMA,
                pltpu.SemaphoreType.DMA,
                pltpu.SemaphoreType.DMA((n_snap - 1,)),
                pltpu.SemaphoreType.DMA((n_snap - 1,)),
                pltpu.SemaphoreType.DMA((chips - 1,)),
                pltpu.SemaphoreType.DMA((chips - 1,)),
                pltpu.SemaphoreType.DMA((n_snap - 1,)),
                pltpu.SemaphoreType.DMA((n_snap - 1,)),
            ]
        scratch += [pltpu.VMEM((n_snap, quarter, 128), F32)]
        grads = [
            jax.ShapeDtypeStruct((9, shard_c, hidden_channels), F32),
            jax.ShapeDtypeStruct((9, shard_h, channels), F32),
            jax.ShapeDtypeStruct((1, shard_h), F32),
            jax.ShapeDtypeStruct((1, shard_c), F32),
        ]
    else:
        grads = [
            jax.ShapeDtypeStruct((9, channels, hidden_channels), F32),
            jax.ShapeDtypeStruct((9, hidden_channels, channels), F32),
            jax.ShapeDtypeStruct((1, hidden_channels), F32),
            jax.ShapeDtypeStruct((1, channels), F32),
        ]
    vmem = pl.BlockSpec(memory_space=pltpu.VMEM)
    results = pl.pallas_call(
        functools.partial(kernel, n_space, n_snap, fused, scale),
        out_shape=[jax.ShapeDtypeStruct((cells, channels), BF16)] * 2 + grads,
        in_specs=[pl.BlockSpec(memory_space=pl.ANY)] * 7,
        out_specs=[pl.BlockSpec(memory_space=pl.ANY)] * 2 + [vmem] * 4,
        scratch_shapes=scratch,
        compiler_params=pltpu.CompilerParams(
            collective_id=0, has_side_effects=True, vmem_limit_bytes=60 * 1024 * 1024
        ),
    )(
        field_in.reshape(cells, channels),
        ocean_mask.reshape(tall, wide),
        cotangent.reshape(cells, channels),
        w_first.reshape(3, 3 * channels, hidden_channels),
        b_first.reshape(1, hidden_channels),
        w_second.reshape(3, 3 * hidden_channels, channels),
        b_second.reshape(1, channels),
    )
    field_out, grad_field, gw1, gw2, gb1, gb2 = pl.pallas_call(
        store_all,
        out_shape=[jax.ShapeDtypeStruct(value.shape, value.dtype) for value in results],
        in_specs=[pl.BlockSpec(memory_space=pl.ANY)] * 6,
        out_specs=[pl.BlockSpec(memory_space=pl.ANY)] * 6,
        scratch_shapes=[pltpu.SemaphoreType.DMA((6,))],
    )(*results)
    whole_shape = field_in.shape
    if not fused:
        sums = (
            lax.psum_scatter(gw1, "space", scatter_dimension=1, tiled=True),
            lax.psum_scatter(gw2, "space", scatter_dimension=1, tiled=True),
            lax.psum_scatter(gb1[0], "space", scatter_dimension=0, tiled=True),
            lax.psum_scatter(gb2[0], "space", scatter_dimension=0, tiled=True),
        )
        gw1, gw2, gb1, gb2 = [value * scale for value in lax.psum(sums, "snap")]
    return (
        field_out.reshape(whole_shape),
        grad_field.reshape(whole_shape),
        gw1.reshape(3, 3, shard_c, hidden_channels),
        gw2.reshape(3, 3, shard_h, channels),
        gb1.reshape(shard_h),
        gb2.reshape(shard_c),
    )


def solution(mesh):
    placed = (
        P("snap", "space", None, None, None),
        P("space", None, None),
        P("snap", "space", None, None, None),
        P(),
        P(),
        P(),
        P(),
    )
    return jax.shard_map(
        local,
        mesh=mesh,
        in_specs=placed,
        out_specs=(
            P("snap", "space", None, None, None),
            P("snap", "space", None, None, None),
            P(None, None, "space", None),
            P(None, None, "space", None),
            P("space"),
            P("space"),
        ),
        check_vma=False,
    )
```

```python
import functools
import math

import jax
import jax.numpy as jnp
from jax import lax
from jax.experimental import pallas as pl
from jax.experimental.pallas import tpu as pltpu
from jax.sharding import PartitionSpec as P

DEV_COLS = 4
ROOT_HALF = 0.7071067811865476
INV_ROOT_TWO_PI = 0.3989422804014327
MESH = pl.DeviceIdType.MESH
F32 = jnp.float32
BF16 = jnp.bfloat16

DIRS = ((-1, 0), (1, 0), (0, -1), (0, 1), (-1, -1), (-1, 1), (1, -1), (1, 1))
UP, DOWN, LEFT, RIGHT, UP_LEFT, UP_RIGHT, DOWN_LEFT, DOWN_RIGHT = range(8)
OPPOSITE = (DOWN, UP, RIGHT, LEFT, DOWN_RIGHT, DOWN_LEFT, UP_RIGHT, UP_LEFT)

WIDE = 32
TALL = 32
CELLS = TALL * WIDE
BAND = 2 * WIDE
BLOCK = 8 * WIDE
BLOCKS = CELLS // BLOCK
STEP = CELLS // 2
EDGE = 2 * TALL
PART = 16


def mm(a, b, dims=(((1,), (0,)), ((), ()))):
    return lax.dot_general(a, b, dims, preferred_element_type=F32)


NT = (((1,), (1,)), ((), ()))
TN = (((0,), (0,)), ((), ()))


def grid2(rows, columns):
    return (
        lax.broadcasted_iota(jnp.int32, (rows, columns), 0),
        lax.broadcasted_iota(jnp.int32, (rows, columns), 1),
    )


def onehot(condition):
    return jnp.where(condition, 1.0, 0.0).astype(BF16)


def shift_left_source(rows):
    r, c = grid2(rows, rows)
    return onehot((c == r - 2) & ((r & (WIDE - 1)) >= 2))


def shift_right_source(rows):
    r, c = grid2(rows, rows)
    return onehot((c == r + 2) & ((r & (WIDE - 1)) < WIDE - 2))


def left_insert(rows, first):
    r, h = grid2(rows, PART)
    x = r & (WIDE - 1)
    return onehot((x < 2) & (h == first + 2 * (r >> 5) + x))


def right_insert(rows, first):
    r, h = grid2(rows, PART)
    x = r & (WIDE - 1)
    return onehot((x >= WIDE - 2) & (h == first + 2 * (r >> 5) + x - (WIDE - 2)))


def left_pack():
    h, r = grid2(PART, BLOCK)
    x = r & (WIDE - 1)
    return onehot((x < 2) & (h == 2 * (r >> 5) + x))


def right_pack():
    h, r = grid2(PART, BLOCK)
    x = r & (WIDE - 1)
    return onehot((x >= WIDE - 2) & (h == 2 * (r >> 5) + x - (WIDE - 2)))


def rows_of(index, size, offset=0):
    return pl.ds(pl.multiple_of(index * size + offset, 16), size)


class Halo:
    def __init__(self, geometry, own, packs, bands, corners, send_sem, recv_sem):
        self.exists, self.peer = geometry
        self.own, self.packs, self.bands, self.corners = own, packs, bands, corners
        sources = (
            own.at[pl.ds(0, BAND)],
            own.at[pl.ds(CELLS - BAND, BAND)],
            packs.at[0],
            packs.at[1],
            packs.at[0, pl.ds(0, PART)],
            packs.at[1, pl.ds(0, PART)],
            packs.at[0, pl.ds(EDGE - PART, PART)],
            packs.at[1, pl.ds(EDGE - PART, PART)],
        )
        self.copies = []
        for d in range(8):
            slot = OPPOSITE[d]
            self.copies.append(
                pltpu.make_async_remote_copy(
                    src_ref=sources[d],
                    dst_ref=self.slot(slot),
                    send_sem=send_sem.at[d],
                    recv_sem=recv_sem.at[slot],
                    device_id={"space": self.peer[d]},
                    device_id_type=MESH,
                )
            )

    def slot(self, slot):
        return self.bands.at[slot] if slot < 4 else self.corners.at[slot - 4]

    def clear_missing(self):
        for d in range(8):
            ref = self.slot(d)

            @pl.when(jnp.logical_not(self.exists[d]))
            def _():
                ref[...] = jnp.zeros(ref.shape, ref.dtype)

    def pack(self):
        to_left, to_right = left_pack(), right_pack()
        for i in range(BLOCKS):
            cells = self.own[pl.ds(i * BLOCK, BLOCK), :]
            self.packs[0, pl.ds(i * PART, PART), :] = mm(to_left, cells).astype(BF16)
            self.packs[1, pl.ds(i * PART, PART), :] = mm(to_right, cells).astype(BF16)

    def start(self):
        for d in range(8):

            @pl.when(self.exists[d])
            def _():
                self.copies[d].start()

    def wait_recv(self):
        for d in range(8):

            @pl.when(self.exists[OPPOSITE[d]])
            def _():
                self.copies[d].wait_recv()

    def wait_send(self):
        for d in range(8):

            @pl.when(self.exists[d])
            def _():
                self.copies[d].wait_send()

    def interior(self, out):
        width = self.own.shape[1]
        from_left, from_right = shift_left_source(BLOCK), shift_right_source(BLOCK)

        def body(i, carry):
            cells = self.own[rows_of(i, BLOCK), :]
            there = rows_of(i, BLOCK, BAND)
            out[there, pl.ds(0, width)] = mm(from_left, cells).astype(BF16)
            out[there, pl.ds(width, width)] = cells
            out[there, pl.ds(2 * width, width)] = mm(from_right, cells).astype(BF16)
            return carry

        lax.fori_loop(0, BLOCKS, body, 0)

    def borders(self, out):
        width = self.own.shape[1]
        into_left, into_right = left_insert(BLOCK, 0), right_insert(BLOCK, 0)

        def body(i, carry):
            there = rows_of(i, BLOCK, BAND)
            for into, side, b in ((into_left, LEFT, 0), (into_right, RIGHT, 2)):
                lanes = pl.ds(b * width, width)
                edge = mm(into, self.bands[side, rows_of(i, PART), :]).astype(BF16)
                out[there, lanes] = out[there, lanes] + edge
            return carry

        lax.fori_loop(0, BLOCKS, body, 0)
        from_left, from_right = shift_left_source(BAND), shift_right_source(BAND)
        for band, first, where, side in (
            (UP, PART - 4, 0, (UP_LEFT, UP_RIGHT)),
            (DOWN, 0, CELLS + BAND, (DOWN_LEFT, DOWN_RIGHT)),
        ):
            cells = self.bands[band]
            rows = pl.ds(where, BAND)
            out[rows, pl.ds(0, width)] = (
                mm(from_left, cells) + mm(left_insert(BAND, first), self.corners[side[0] - 4])
            ).astype(BF16)
            out[rows, pl.ds(width, width)] = cells
            out[rows, pl.ds(2 * width, width)] = (
                mm(from_right, cells) + mm(right_insert(BAND, first), self.corners[side[1] - 4])
            ).astype(BF16)


class Reduction:
    def __init__(self, n_space, n_snap, share, a_in, q, b_in, t, c_in, u, d_in, sems):
        self.n_chip, self.n_snap = n_space // 2, n_snap
        self.share, self.a_in, self.q, self.b_in = share, a_in, q, b_in
        self.t, self.c_in, self.u, self.d_in = t, c_in, u, d_in
        me = lax.axis_index("space")
        snap = lax.axis_index("snap")
        self.core = lax.rem(me, 2)
        self.chip = lax.div(me, 2)
        self.snap = snap
        a_s, a_r, b_s, b_r, c_s, c_r, d_s, d_r = sems

        def copy(src, dst, send, recv, device):
            return pltpu.make_async_remote_copy(
                src_ref=src,
                dst_ref=dst,
                send_sem=send,
                recv_sem=recv,
                device_id=device,
                device_id_type=MESH,
            )

        self.a = [copy(share.at[1 - self.core], a_in, a_s, a_r, {"space": me + 1 - 2 * self.core})]
        self.b, self.c, self.d = [], [], []
        for j in range(1, n_snap):
            other = lax.rem(snap + j, n_snap)
            self.b.append(
                copy(q.at[other], b_in.at[j - 1], b_s.at[j - 1], b_r.at[j - 1], {"snap": other})
            )
            self.d.append(
                copy(u, d_in.at[j - 1], d_s.at[j - 1], d_r.at[j - 1], {"snap": other})
            )
        for j in range(1, self.n_chip):
            other = lax.rem(self.chip + j, self.n_chip)
            self.c.append(
                copy(
                    t.at[other],
                    c_in.at[j - 1],
                    c_s.at[j - 1],
                    c_r.at[j - 1],
                    {"space": 2 * other + self.core},
                )
            )

    def start_a(self):
        self.a[0].start()

    def start_b(self):
        self.a[0].wait_recv()
        for z in range(self.n_chip):
            for k in range(self.n_snap):
                both = self.share[self.core, z, k].astype(F32) + self.a_in[z, k].astype(F32)
                self.q[k, z] = both.astype(BF16)
        for c in self.b:
            c.start()

    def start_c(self):
        for c in self.b:
            c.wait_recv()
        for z in range(self.n_chip):
            total = self.q[self.snap, z].astype(F32)
            for j in range(self.n_snap - 1):
                total += self.b_in[j, z].astype(F32)
            self.t[z] = total.astype(BF16)
        for c in self.c:
            c.start()

    def start_d(self):
        for c in self.c:
            c.wait_recv()
        total = self.t[self.chip].astype(F32)
        for j in range(self.n_chip - 1):
            total += self.c_in[j].astype(F32)
        self.u[...] = total.astype(BF16)
        for c in self.d:
            c.start()

    def finish(self, scale, whole):
        for c in self.d:
            c.wait_recv()
        whole[self.snap] = self.u[...].astype(F32) * scale
        for j in range(1, self.n_snap):
            sender = lax.rem(self.snap + self.n_snap - j, self.n_snap)
            whole[sender] = self.d_in[j - 1].astype(F32) * scale

    def wait_send(self):
        for c in self.a + self.b + self.c + self.d:
            c.wait_send()


def kernel(n_space, n_snap, fused, scale, *refs):
    refs = list(refs)

    def take(count):
        got = refs[:count]
        del refs[:count]
        return got

    sources = take(7)
    field_dst, grad_dst, gw1, gw2, gb1, gb2 = take(6)
    halo_refs = [take(6) for _ in range(4)]
    f3, g3, h3, p3 = take(4)
    mfull, mslope, hall, pall, w1t, w2t = take(6)
    mask, cot, w1, b1, w2, b2, load_sem = take(7)
    field_out, grad_field, store_sem = take(3)
    stores = [
        pltpu.make_async_copy(field_out, field_dst, store_sem.at[0]),
        pltpu.make_async_copy(grad_field, grad_dst, store_sem.at[1]),
    ]
    field, mixed_grad, hidden_ref, pre_grad = [group[0] for group in halo_refs]
    channels, hidden_channels = cot.shape[1], hidden_ref.shape[1]
    loads = [
        pltpu.make_async_copy(src, dst, load_sem.at[n])
        for n, (src, dst) in enumerate(zip(sources, (field, mask, cot, w1, b1, w2, b2)))
    ]
    for n in (0, 1, 2, 3, 5, 4, 6):
        loads[n].start()

    me = lax.axis_index("space")
    position = lax.rem(me + 1, n_space)
    line, column = lax.div(position, DEV_COLS), lax.rem(position, DEV_COLS)
    lines = n_space // DEV_COLS
    exists, peer = [], []
    for dy, dx in DIRS:
        there = None
        if dy:
            there = (line > 0) if dy < 0 else (line < lines - 1)
        if dx:
            inside = (column > 0) if dx < 0 else (column < DEV_COLS - 1)
            there = inside if there is None else jnp.logical_and(there, inside)
        exists.append(there)
        peer.append(lax.rem(position + DEV_COLS * dy + dx - 1 + 2 * n_space, n_space))
    geometry = (exists, peer)

    reductions = []
    if fused:
        for _ in range(2):
            share, a_in, q, b_in, t, c_in, u, d_in = take(8)
            sems = take(8)
            reductions.append(
                Reduction(n_space, n_snap, share, a_in, q, b_in, t, c_in, u, d_in, sems)
            )
        (whole,) = take(1)

    halos = [Halo(geometry, *group) for group in halo_refs]
    of_field, of_mixed, of_hidden, of_pre = halos

    barrier = pltpu.get_barrier_semaphore()
    expected = jnp.int32(0)
    for d in range(8):

        @pl.when(exists[d])
        def _():
            pl.semaphore_signal(barrier, inc=1, device_id={"space": peer[d]}, device_id_type=MESH)

        expected = expected + exists[d].astype(jnp.int32)
    if fused:
        core = lax.rem(me, 2)
        pl.semaphore_signal(
            barrier, inc=1, device_id={"space": me + 1 - 2 * core}, device_id_type=MESH
        )
        for j in range(1, n_snap):
            other = lax.rem(lax.axis_index("snap") + j, n_snap)
            pl.semaphore_signal(barrier, inc=1, device_id={"snap": other}, device_id_type=MESH)
        for j in range(1, n_space // 2):
            other = lax.rem(lax.div(me, 2) + j, n_space // 2)
            pl.semaphore_signal(
                barrier, inc=1, device_id={"space": 2 * other + core}, device_id_type=MESH
            )
        expected = expected + (1 + n_snap - 1 + n_space // 2 - 1)

    for halo in halos:
        halo.clear_missing()
    loads[0].wait()
    of_field.pack()
    pl.semaphore_wait(barrier, expected)
    of_field.start()
    loads[1].wait()
    loads[2].wait()

    mask_bits = mask[...].astype(F32).astype(BF16)

    def prepare(i, carry):
        here = rows_of(i, BLOCK)
        r, y = grid2(BLOCK, TALL)
        lines_of = mm(onehot((r >> 5) + i * (BLOCK // WIDE) == y), mask_bits)
        r, x = grid2(BLOCK, WIDE)
        one = jnp.where((r & (WIDE - 1)) == x, lines_of, 0.0).astype(BF16)
        m = mm(one, jnp.ones((WIDE, 128), BF16))
        mfull[here, :] = m
        for half in range(channels // 128):
            lanes = pl.ds(half * 128, 128)
            mixed_grad[here, lanes] = (
                cot[here, lanes].astype(F32) * m
            ).astype(BF16)
        return carry

    lax.fori_loop(0, BLOCKS, prepare, 0)
    of_mixed.pack()
    of_mixed.start()
    of_field.interior(f3)
    for n in (3, 4, 5, 6):
        loads[n].wait()
    for a in range(3):
        for b in range(3):
            w2t[a, pl.ds(b * channels, channels), :] = w2[
                2 - a, pl.ds((2 - b) * hidden_channels, hidden_channels), :
            ].T
            w1t[a, pl.ds(b * hidden_channels, hidden_channels), :] = w1[
                2 - a, pl.ds((2 - b) * channels, channels), :
            ].T
    pad = jnp.zeros((BAND, hidden_channels), BF16)
    for buf in (hall, pall):
        for a in range(3):
            for b in range(3):
                if a != b:
                    where = BAND * b if b < a else CELLS + BAND * (b - 1)
                    buf[pl.ds(where, BAND), pl.ds(a * hidden_channels, hidden_channels)] = pad
    of_mixed.interior(g3)
    of_field.wait_recv()
    of_field.borders(f3)

    def hidden_part(i, carry):
        here = rows_of(i, STEP)
        pre = jnp.zeros((STEP, hidden_channels), F32)
        for a in range(3):
            pre += mm(f3[rows_of(i, STEP, BAND * a), :], w1[a])
        pre = pre + b1[...]
        m = mfull[here, :]
        bell = 0.5 * (1.0 + lax.erf(pre * ROOT_HALF))
        hidden = (m * (pre * bell)).astype(BF16)
        mslope[here, :] = m * (bell + pre * jnp.exp(-0.5 * pre * pre) * INV_ROOT_TWO_PI)
        hidden_ref[here, :] = hidden
        for a in range(3):
            hall[rows_of(i, STEP, BAND * a), pl.ds(a * hidden_channels, hidden_channels)] = hidden
        return carry

    lax.fori_loop(0, CELLS // STEP, hidden_part, 0)
    of_hidden.pack()
    of_hidden.start()
    of_mixed.wait_recv()
    of_mixed.borders(g3)

    def pre_grad_part(i, carry):
        here = rows_of(i, STEP)
        g_hidden = jnp.zeros((STEP, hidden_channels), F32)
        for a in range(3):
            g_hidden += mm(g3[rows_of(i, STEP, BAND * a), :], w2t[a])
        g_pre = (g_hidden * mslope[here, :]).astype(BF16)
        pre_grad[here, :] = g_pre
        for a in range(3):
            pall[rows_of(i, STEP, BAND * a), pl.ds(a * hidden_channels, hidden_channels)] = g_pre
        return carry

    ones = jnp.ones((PART, CELLS), BF16)
    if fused:
        shard_c, shard_h = channels // n_space, hidden_channels // n_space
        share0, share1 = reductions[0].share, reductions[1].share
        quarter = share0.shape[3]

        def put(share, s, row, value):
            done = 0
            count = value.shape[0]
            while done < count:
                at = row + done
                k, within = at // quarter, at % quarter
                size = min(count - done, quarter - within)
                share[s % 2, s // 2, k, pl.ds(within, size), :] = value[done : done + size]
                done += size

        halves = channels // 128
        rows2 = 9 * shard_h * halves
        all_sums = mm(hall[...], g3[...], TN).astype(BF16)
        for b in range(3):
            sums = all_sums[:, (2 - b) * channels : (3 - b) * channels]
            for a in range(3):
                part = sums[(2 - a) * hidden_channels : (3 - a) * hidden_channels]
                t = 3 * a + b
                for s in range(n_space):
                    for half in range(halves):
                        put(
                            share0,
                            s,
                            (t * halves + half) * shard_h,
                            part[s * shard_h : (s + 1) * shard_h, half * 128 : half * 128 + 128],
                        )
        for s in range(n_space):
            left = n_snap * quarter - rows2
            if left:
                put(share0, s, rows2, jnp.zeros((left, 128), BF16))
        reductions[0].start_a()

        lax.fori_loop(0, CELLS // STEP, pre_grad_part, 0)
        of_pre.pack()
        of_pre.start()
        reductions[0].start_b()

        rows1 = 9 * shard_c
        r, _ = grid2(PART, 128)
        sum_pre = mm(ones, pre_grad[...])
        sum_mixed = mm(ones, mixed_grad[...])
        biases = jnp.where(
            r == 0,
            sum_pre,
            jnp.where(r == 1, sum_mixed[:, :128], jnp.where(r == 2, sum_mixed[:, 128:], 0.0)),
        ).astype(BF16)
        for s in range(n_space):
            put(share1, s, rows1, biases)
            left = n_snap * quarter - rows1 - PART
            if left:
                put(share1, s, rows1 + PART, jnp.zeros((left, 128), BF16))
        all_sums = mm(pall[...], f3[...], TN)
        for b in range(3):
            sums = all_sums[:, b * channels : (b + 1) * channels]
            for a in range(3):
                part = sums[a * hidden_channels : (a + 1) * hidden_channels].T.astype(BF16)
                t = 3 * a + b
                for s in range(n_space):
                    put(share1, s, t * shard_c, part[s * shard_c : (s + 1) * shard_c])
        reductions[1].start_a()
    else:
        lax.fori_loop(0, CELLS // STEP, pre_grad_part, 0)
        of_pre.pack()
        of_pre.start()
        sum_pre = mm(ones, pre_grad[...])
        sum_mixed = mm(ones, mixed_grad[...])
        for b in range(3):
            sums = mm(hall[...], g3[:, pl.ds((2 - b) * channels, channels)], TN)
            for a in range(3):
                gw2[3 * a + b] = sums[(2 - a) * hidden_channels : (3 - a) * hidden_channels]
            sums = mm(pall[...], f3[:, pl.ds(b * channels, channels)], TN)
            for a in range(3):
                gw1[3 * a + b] = sums[a * hidden_channels : (a + 1) * hidden_channels].T
        gb1[...] = sum_pre[0:1]
        gb2[...] = sum_mixed[0:1]

    of_hidden.interior(h3)
    of_pre.interior(p3)
    if fused:
        reductions[1].start_b()
    of_hidden.wait_recv()
    of_hidden.borders(h3)

    def out_part(i, carry):
        here = rows_of(i, STEP)
        mixed = jnp.zeros((STEP, channels), F32)
        for a in range(3):
            mixed += mm(h3[rows_of(i, STEP, BAND * a), :], w2[a])
        mixed = mixed + b2[...]
        m = mfull[here, :]
        for half in range(channels // 128):
            lanes = pl.ds(half * 128, 128)
            field_out[here, lanes] = (
                field[here, lanes].astype(F32) + m * mixed[:, half * 128 : half * 128 + 128]
            ).astype(BF16)
        return carry

    def grad_part(i, carry):
        here = rows_of(i, STEP)
        total = jnp.zeros((STEP, channels), F32)
        for a in range(3):
            total += mm(p3[rows_of(i, STEP, BAND * a), :], w1t[a])
        grad_field[here, :] = (cot[here, :].astype(F32) + total).astype(BF16)
        return carry

    lax.fori_loop(0, CELLS // STEP, out_part, 0)
    stores[0].start()
    if fused:
        reductions[0].start_c()
    of_pre.wait_recv()
    of_pre.borders(p3)
    lax.fori_loop(0, CELLS // STEP, grad_part, 0)
    stores[1].start()
    if fused:
        reductions[0].start_d()
        reductions[1].start_c()
        reductions[0].finish(scale, whole)

        def get(row, count):
            pieces = []
            done = 0
            while done < count:
                at = row + done
                k, within = at // quarter, at % quarter
                size = min(count - done, quarter - within)
                pieces.append(whole[k, pl.ds(within, size), :])
                done += size
            return pieces[0] if len(pieces) == 1 else jnp.concatenate(pieces, axis=0)

        for t in range(9):
            for half in range(halves):
                gw2[t, :, pl.ds(half * 128, 128)] = get((t * halves + half) * shard_h, shard_h)
        reductions[1].start_d()
        reductions[1].finish(scale, whole)
        tail = get(rows1, PART)
        r, c = grid2(128, shard_h)
        pick = jnp.where(r == c + me * shard_h, 1.0, 0.0)
        gb1[...] = jnp.dot(
            tail, pick, preferred_element_type=F32, precision=lax.Precision.HIGHEST
        )[0:1]
        picked = jnp.zeros((PART, shard_c), F32)
        for half in range(halves):
            r, c = grid2(128, shard_c)
            pick = jnp.where(r + half * 128 == c + me * shard_c, 1.0, 0.0)
            picked = picked + jnp.where(
                lax.broadcasted_iota(jnp.int32, (PART, shard_c), 0) == 1 + half,
                jnp.dot(tail, pick, preferred_element_type=F32, precision=lax.Precision.HIGHEST),
                0.0,
            )
        gb2[...] = jnp.sum(picked, axis=0, keepdims=True)
        for t in range(9):
            gw1[t] = get(t * shard_c, shard_c)
        for red in reductions:
            red.wait_send()
    for halo in halos:
        halo.wait_send()
    for c in stores:
        c.wait()


def store_all(count, *refs):
    ins, outs, held, in_sem, out_sem = (
        refs[:count],
        refs[count : 2 * count],
        refs[2 * count : 3 * count],
        refs[-2],
        refs[-1],
    )
    pieces = []
    for n in range(count):
        rows = ins[n].shape[0]
        parts = 4 if rows % 64 == 0 else 1
        for k in range(parts):
            where = pl.ds(k * (rows // parts), rows // parts)
            i = len(pieces)
            pieces.append(
                (
                    pltpu.make_async_copy(ins[n].at[where], held[n].at[where], in_sem.at[i]),
                    pltpu.make_async_copy(held[n].at[where], outs[n].at[where], out_sem.at[i]),
                )
            )
    for load, _ in pieces:
        load.start()
    for load, store in pieces:
        load.wait()
        store.start()
    for _, store in pieces:
        store.wait()


def local(field_in, ocean_mask, cotangent, w_first, b_first, w_second, b_second):
    n_space, n_snap = lax.axis_size("space"), lax.axis_size("snap")
    tall, wide, channels = field_in.shape[2:]
    hidden_channels = w_first.shape[3]
    total = field_in.shape[0] * n_snap * n_space * tall * wide
    scale = 1.0 / math.sqrt(float(total))
    cells = tall * wide
    shard_c, shard_h = channels // n_space, hidden_channels // n_space
    fused = shard_c % 16 == 0 and shard_h % 16 == 0

    def halo_scratch(width):
        return [
            pltpu.VMEM((cells, width), BF16),
            pltpu.VMEM((2, EDGE, width), BF16),
            pltpu.VMEM((4, BAND, width), BF16),
            pltpu.VMEM((4, PART, width), BF16),
            pltpu.SemaphoreType.DMA((8,)),
            pltpu.SemaphoreType.DMA((8,)),
        ]

    widths = (channels, channels, hidden_channels, hidden_channels)
    scratch = []
    for width in widths:
        scratch += halo_scratch(width)
    scratch += [pltpu.VMEM((cells + 2 * BAND, 3 * width), BF16) for width in widths]
    scratch += [
        pltpu.VMEM((cells, 128), F32),
        pltpu.VMEM((cells, hidden_channels), F32),
        pltpu.VMEM((cells + 2 * BAND, 3 * hidden_channels), BF16),
        pltpu.VMEM((cells + 2 * BAND, 3 * hidden_channels), BF16),
        pltpu.VMEM((3, 3 * hidden_channels, channels), BF16),
        pltpu.VMEM((3, 3 * channels, hidden_channels), BF16),
        pltpu.VMEM((tall, wide), jnp.int32),
        pltpu.VMEM((cells, channels), BF16),
        pltpu.VMEM((3, 3 * channels, hidden_channels), BF16),
        pltpu.VMEM((1, hidden_channels), F32),
        pltpu.VMEM((3, 3 * hidden_channels, channels), BF16),
        pltpu.VMEM((1, channels), F32),
        pltpu.SemaphoreType.DMA((7,)),
        pltpu.VMEM((cells, channels), BF16),
        pltpu.VMEM((cells, channels), BF16),
        pltpu.SemaphoreType.DMA((2,)),
    ]
    if fused:
        chips = n_space // 2
        need = max(9 * shard_c * hidden_channels // 128 + PART, 9 * shard_h * channels // 128)
        quarter = -(-need // (PART * n_snap)) * PART
        for _ in range(2):
            piece = (quarter, 128)
            scratch += [
                pltpu.VMEM((2, chips, n_snap) + piece, BF16),
                pltpu.VMEM((chips, n_snap) + piece, BF16),
                pltpu.VMEM((n_snap, chips) + piece, BF16),
                pltpu.VMEM((n_snap - 1, chips) + piece, BF16),
                pltpu.VMEM((chips,) + piece, BF16),
                pltpu.VMEM((chips - 1,) + piece, BF16),
                pltpu.VMEM(piece, BF16),
                pltpu.VMEM((n_snap - 1,) + piece, BF16),
                pltpu.SemaphoreType.DMA,
                pltpu.SemaphoreType.DMA,
                pltpu.SemaphoreType.DMA((n_snap - 1,)),
                pltpu.SemaphoreType.DMA((n_snap - 1,)),
                pltpu.SemaphoreType.DMA((chips - 1,)),
                pltpu.SemaphoreType.DMA((chips - 1,)),
                pltpu.SemaphoreType.DMA((n_snap - 1,)),
                pltpu.SemaphoreType.DMA((n_snap - 1,)),
            ]
        scratch += [pltpu.VMEM((n_snap, quarter, 128), F32)]
        grads = [
            jax.ShapeDtypeStruct((9, shard_c, hidden_channels), F32),
            jax.ShapeDtypeStruct((9, shard_h, channels), F32),
            jax.ShapeDtypeStruct((1, shard_h), F32),
            jax.ShapeDtypeStruct((1, shard_c), F32),
        ]
    else:
        grads = [
            jax.ShapeDtypeStruct((9, channels, hidden_channels), F32),
            jax.ShapeDtypeStruct((9, hidden_channels, channels), F32),
            jax.ShapeDtypeStruct((1, hidden_channels), F32),
            jax.ShapeDtypeStruct((1, channels), F32),
        ]
    vmem = pl.BlockSpec(memory_space=pltpu.VMEM)
    results = pl.pallas_call(
        functools.partial(kernel, n_space, n_snap, fused, scale),
        out_shape=[jax.ShapeDtypeStruct((cells, channels), BF16)] * 2 + grads,
        in_specs=[pl.BlockSpec(memory_space=pl.ANY)] * 7,
        out_specs=[pl.BlockSpec(memory_space=pl.ANY)] * 2 + [vmem] * 4,
        scratch_shapes=scratch,
        compiler_params=pltpu.CompilerParams(
            collective_id=0, has_side_effects=True, vmem_limit_bytes=60 * 1024 * 1024
        ),
    )(
        field_in.reshape(cells, channels),
        ocean_mask.reshape(tall, wide),
        cotangent.reshape(cells, channels),
        w_first.reshape(3, 3 * channels, hidden_channels),
        b_first.reshape(1, hidden_channels),
        w_second.reshape(3, 3 * hidden_channels, channels),
        b_second.reshape(1, channels),
    )
    field_out, grad_field, gw1, gw2, gb1, gb2 = pl.pallas_call(
        functools.partial(store_all, 6),
        out_shape=[jax.ShapeDtypeStruct(value.shape, value.dtype) for value in results],
        in_specs=[pl.BlockSpec(memory_space=pl.ANY)] * 6,
        out_specs=[pl.BlockSpec(memory_space=pl.ANY)] * 6,
        scratch_shapes=[pltpu.VMEM(value.shape, value.dtype) for value in results]
        + [pltpu.SemaphoreType.DMA((12,)), pltpu.SemaphoreType.DMA((12,))],
        compiler_params=pltpu.CompilerParams(vmem_limit_bytes=60 * 1024 * 1024),
    )(*results)
    whole_shape = field_in.shape
    if not fused:
        sums = (
            lax.psum_scatter(gw1, "space", scatter_dimension=1, tiled=True),
            lax.psum_scatter(gw2, "space", scatter_dimension=1, tiled=True),
            lax.psum_scatter(gb1[0], "space", scatter_dimension=0, tiled=True),
            lax.psum_scatter(gb2[0], "space", scatter_dimension=0, tiled=True),
        )
        gw1, gw2, gb1, gb2 = [value * scale for value in lax.psum(sums, "snap")]
    return (
        field_out.reshape(whole_shape),
        grad_field.reshape(whole_shape),
        gw1.reshape(3, 3, shard_c, hidden_channels),
        gw2.reshape(3, 3, shard_h, channels),
        gb1.reshape(shard_h),
        gb2.reshape(shard_c),
    )


def solution(mesh):
    placed = (
        P("snap", "space", None, None, None),
        P("space", None, None),
        P("snap", "space", None, None, None),
        P(),
        P(),
        P(),
        P(),
    )
    return jax.shard_map(
        local,
        mesh=mesh,
        in_specs=placed,
        out_specs=(
            P("snap", "space", None, None, None),
            P("snap", "space", None, None, None),
            P(None, None, "space", None),
            P(None, None, "space", None),
            P("space"),
            P("space"),
        ),
        check_vma=False,
    )
```

```python
import functools
import math

import jax
import jax.numpy as jnp
from jax import lax
from jax.experimental import pallas as pl
from jax.experimental.pallas import tpu as pltpu
from jax.sharding import PartitionSpec as P

DEV_COLS = 4
ROOT_HALF = 0.7071067811865476
INV_ROOT_TWO_PI = 0.3989422804014327
MESH = pl.DeviceIdType.MESH
F32 = jnp.float32
BF16 = jnp.bfloat16

DIRS = ((-1, 0), (1, 0), (0, -1), (0, 1), (-1, -1), (-1, 1), (1, -1), (1, 1))
UP, DOWN, LEFT, RIGHT, UP_LEFT, UP_RIGHT, DOWN_LEFT, DOWN_RIGHT = range(8)
OPPOSITE = (DOWN, UP, RIGHT, LEFT, DOWN_RIGHT, DOWN_LEFT, UP_RIGHT, UP_LEFT)

WIDE = 32
TALL = 32
CELLS = TALL * WIDE
BAND = 2 * WIDE
BLOCK = 8 * WIDE
BLOCKS = CELLS // BLOCK
STEP = CELLS // 2
EDGE = 2 * TALL
PART = 16


def mm(a, b, dims=(((1,), (0,)), ((), ()))):
    return lax.dot_general(a, b, dims, preferred_element_type=F32)


NT = (((1,), (1,)), ((), ()))
TN = (((0,), (0,)), ((), ()))


def grid2(rows, columns):
    return (
        lax.broadcasted_iota(jnp.int32, (rows, columns), 0),
        lax.broadcasted_iota(jnp.int32, (rows, columns), 1),
    )


def onehot(condition):
    return jnp.where(condition, 1.0, 0.0).astype(BF16)


def shift_left_source(rows):
    r, c = grid2(rows, rows)
    return onehot((c == r - 2) & ((r & (WIDE - 1)) >= 2))


def shift_right_source(rows):
    r, c = grid2(rows, rows)
    return onehot((c == r + 2) & ((r & (WIDE - 1)) < WIDE - 2))


def left_insert(rows, first):
    r, h = grid2(rows, PART)
    x = r & (WIDE - 1)
    return onehot((x < 2) & (h == first + 2 * (r >> 5) + x))


def right_insert(rows, first):
    r, h = grid2(rows, PART)
    x = r & (WIDE - 1)
    return onehot((x >= WIDE - 2) & (h == first + 2 * (r >> 5) + x - (WIDE - 2)))


def left_pack():
    h, r = grid2(PART, BLOCK)
    x = r & (WIDE - 1)
    return onehot((x < 2) & (h == 2 * (r >> 5) + x))


def right_pack():
    h, r = grid2(PART, BLOCK)
    x = r & (WIDE - 1)
    return onehot((x >= WIDE - 2) & (h == 2 * (r >> 5) + x - (WIDE - 2)))


def rows_of(index, size, offset=0):
    return pl.ds(pl.multiple_of(index * size + offset, 16), size)


class Halo:
    def __init__(self, geometry, own, packs, bands, corners, send_sem, recv_sem):
        self.exists, self.peer = geometry
        self.own, self.packs, self.bands, self.corners = own, packs, bands, corners
        sources = (
            own.at[pl.ds(0, BAND)],
            own.at[pl.ds(CELLS - BAND, BAND)],
            packs.at[0],
            packs.at[1],
            packs.at[0, pl.ds(0, PART)],
            packs.at[1, pl.ds(0, PART)],
            packs.at[0, pl.ds(EDGE - PART, PART)],
            packs.at[1, pl.ds(EDGE - PART, PART)],
        )
        self.copies = []
        for d in range(8):
            slot = OPPOSITE[d]
            self.copies.append(
                pltpu.make_async_remote_copy(
                    src_ref=sources[d],
                    dst_ref=self.slot(slot),
                    send_sem=send_sem.at[d],
                    recv_sem=recv_sem.at[slot],
                    device_id={"space": self.peer[d]},
                    device_id_type=MESH,
                )
            )

    def slot(self, slot):
        return self.bands.at[slot] if slot < 4 else self.corners.at[slot - 4]

    def clear_missing(self):
        for d in range(8):
            ref = self.slot(d)

            @pl.when(jnp.logical_not(self.exists[d]))
            def _():
                ref[...] = jnp.zeros(ref.shape, ref.dtype)

    def pack(self):
        to_left, to_right = left_pack(), right_pack()
        for i in range(BLOCKS):
            cells = self.own[pl.ds(i * BLOCK, BLOCK), :]
            self.packs[0, pl.ds(i * PART, PART), :] = mm(to_left, cells).astype(BF16)
            self.packs[1, pl.ds(i * PART, PART), :] = mm(to_right, cells).astype(BF16)

    def start(self):
        for d in range(8):

            @pl.when(self.exists[d])
            def _():
                self.copies[d].start()

    def wait_recv(self):
        for d in range(8):

            @pl.when(self.exists[OPPOSITE[d]])
            def _():
                self.copies[d].wait_recv()

    def wait_send(self):
        for d in range(8):

            @pl.when(self.exists[d])
            def _():
                self.copies[d].wait_send()

    def interior(self, out):
        width = self.own.shape[1]
        from_left, from_right = shift_left_source(BLOCK), shift_right_source(BLOCK)

        def body(i, carry):
            cells = self.own[rows_of(i, BLOCK), :]
            there = rows_of(i, BLOCK, BAND)
            out[there, pl.ds(0, width)] = mm(from_left, cells).astype(BF16)
            out[there, pl.ds(width, width)] = cells
            out[there, pl.ds(2 * width, width)] = mm(from_right, cells).astype(BF16)
            return carry

        lax.fori_loop(0, BLOCKS, body, 0)

    def borders(self, out):
        width = self.own.shape[1]
        into_left, into_right = left_insert(BLOCK, 0), right_insert(BLOCK, 0)

        def body(i, carry):
            there = rows_of(i, BLOCK, BAND)
            for into, side, b in ((into_left, LEFT, 0), (into_right, RIGHT, 2)):
                lanes = pl.ds(b * width, width)
                edge = mm(into, self.bands[side, rows_of(i, PART), :]).astype(BF16)
                out[there, lanes] = out[there, lanes] + edge
            return carry

        lax.fori_loop(0, BLOCKS, body, 0)
        from_left, from_right = shift_left_source(BAND), shift_right_source(BAND)
        for band, first, where, side in (
            (UP, PART - 4, 0, (UP_LEFT, UP_RIGHT)),
            (DOWN, 0, CELLS + BAND, (DOWN_LEFT, DOWN_RIGHT)),
        ):
            cells = self.bands[band]
            rows = pl.ds(where, BAND)
            out[rows, pl.ds(0, width)] = (
                mm(from_left, cells) + mm(left_insert(BAND, first), self.corners[side[0] - 4])
            ).astype(BF16)
            out[rows, pl.ds(width, width)] = cells
            out[rows, pl.ds(2 * width, width)] = (
                mm(from_right, cells) + mm(right_insert(BAND, first), self.corners[side[1] - 4])
            ).astype(BF16)


class Reduction:
    def __init__(self, n_space, n_snap, share, a_in, q, b_in, t, c_in, u, d_in, sems):
        self.n_chip, self.n_snap = n_space // 2, n_snap
        self.share, self.a_in, self.q, self.b_in = share, a_in, q, b_in
        self.t, self.c_in, self.u, self.d_in = t, c_in, u, d_in
        me = lax.axis_index("space")
        snap = lax.axis_index("snap")
        self.core = lax.rem(me, 2)
        self.chip = lax.div(me, 2)
        self.snap = snap
        a_s, a_r, b_s, b_r, c_s, c_r, d_s, d_r = sems

        def copy(src, dst, send, recv, device):
            return pltpu.make_async_remote_copy(
                src_ref=src,
                dst_ref=dst,
                send_sem=send,
                recv_sem=recv,
                device_id=device,
                device_id_type=MESH,
            )

        self.a = [copy(share.at[1 - self.core], a_in, a_s, a_r, {"space": me + 1 - 2 * self.core})]
        self.b, self.c, self.d = [], [], []
        for j in range(1, n_snap):
            other = lax.rem(snap + j, n_snap)
            self.b.append(
                copy(q.at[other], b_in.at[j - 1], b_s.at[j - 1], b_r.at[j - 1], {"snap": other})
            )
            self.d.append(
                copy(u, d_in.at[j - 1], d_s.at[j - 1], d_r.at[j - 1], {"snap": other})
            )
        for j in range(1, self.n_chip):
            other = lax.rem(self.chip + j, self.n_chip)
            self.c.append(
                copy(
                    t.at[other],
                    c_in.at[j - 1],
                    c_s.at[j - 1],
                    c_r.at[j - 1],
                    {"space": 2 * other + self.core},
                )
            )

    def start_a(self):
        self.a[0].start()

    def start_b(self):
        self.a[0].wait_recv()
        for z in range(self.n_chip):
            for k in range(self.n_snap):
                both = self.share[self.core, z, k].astype(F32) + self.a_in[z, k].astype(F32)
                self.q[k, z] = both.astype(BF16)
        for c in self.b:
            c.start()

    def start_c(self):
        for c in self.b:
            c.wait_recv()
        for z in range(self.n_chip):
            total = self.q[self.snap, z].astype(F32)
            for j in range(self.n_snap - 1):
                total += self.b_in[j, z].astype(F32)
            self.t[z] = total.astype(BF16)
        for c in self.c:
            c.start()

    def start_d(self):
        for c in self.c:
            c.wait_recv()
        total = self.t[self.chip].astype(F32)
        for j in range(self.n_chip - 1):
            total += self.c_in[j].astype(F32)
        self.u[...] = total.astype(BF16)
        for c in self.d:
            c.start()

    def finish(self, scale, whole):
        for c in self.d:
            c.wait_recv()
        whole[self.snap] = self.u[...].astype(F32) * scale
        for j in range(1, self.n_snap):
            sender = lax.rem(self.snap + self.n_snap - j, self.n_snap)
            whole[sender] = self.d_in[j - 1].astype(F32) * scale

    def wait_send(self):
        for c in self.a + self.b + self.c + self.d:
            c.wait_send()


def kernel(n_space, n_snap, fused, scale, *refs):
    refs = list(refs)

    def take(count):
        got = refs[:count]
        del refs[:count]
        return got

    sources = take(7)
    field_dst, grad_dst, gw1, gw2, gb1, gb2 = take(6)
    halo_refs = [take(6) for _ in range(4)]
    f3, g3, h3, p3 = take(4)
    mfull, mslope, hall, pall, w1t, w2t = take(6)
    mask, cot, w1, b1, w2, b2, load_sem = take(7)
    field_out, grad_field, store_sem = take(3)
    stores = [
        pltpu.make_async_copy(field_out, field_dst, store_sem.at[0]),
        pltpu.make_async_copy(grad_field, grad_dst, store_sem.at[1]),
    ]
    field, mixed_grad, hidden_ref, pre_grad = [group[0] for group in halo_refs]
    channels, hidden_channels = cot.shape[1], hidden_ref.shape[1]
    loads = [
        pltpu.make_async_copy(src, dst, load_sem.at[n])
        for n, (src, dst) in enumerate(zip(sources, (field, mask, cot, w1, b1, w2, b2)))
    ]
    for n in (0, 1, 2, 3, 5, 4, 6):
        loads[n].start()

    me = lax.axis_index("space")
    position = lax.rem(me + 1, n_space)
    line, column = lax.div(position, DEV_COLS), lax.rem(position, DEV_COLS)
    lines = n_space // DEV_COLS
    exists, peer = [], []
    for dy, dx in DIRS:
        there = None
        if dy:
            there = (line > 0) if dy < 0 else (line < lines - 1)
        if dx:
            inside = (column > 0) if dx < 0 else (column < DEV_COLS - 1)
            there = inside if there is None else jnp.logical_and(there, inside)
        exists.append(there)
        peer.append(lax.rem(position + DEV_COLS * dy + dx - 1 + 2 * n_space, n_space))
    geometry = (exists, peer)

    reductions = []
    if fused:
        for _ in range(2):
            share, a_in, q, b_in, t, c_in, u, d_in = take(8)
            sems = take(8)
            reductions.append(
                Reduction(n_space, n_snap, share, a_in, q, b_in, t, c_in, u, d_in, sems)
            )
        (whole,) = take(1)

    halos = [Halo(geometry, *group) for group in halo_refs]
    of_field, of_mixed, of_hidden, of_pre = halos

    barrier = pltpu.get_barrier_semaphore()
    expected = jnp.int32(0)
    for d in range(8):

        @pl.when(exists[d])
        def _():
            pl.semaphore_signal(barrier, inc=1, device_id={"space": peer[d]}, device_id_type=MESH)

        expected = expected + exists[d].astype(jnp.int32)
    if fused:
        core = lax.rem(me, 2)
        pl.semaphore_signal(
            barrier, inc=1, device_id={"space": me + 1 - 2 * core}, device_id_type=MESH
        )
        for j in range(1, n_snap):
            other = lax.rem(lax.axis_index("snap") + j, n_snap)
            pl.semaphore_signal(barrier, inc=1, device_id={"snap": other}, device_id_type=MESH)
        for j in range(1, n_space // 2):
            other = lax.rem(lax.div(me, 2) + j, n_space // 2)
            pl.semaphore_signal(
                barrier, inc=1, device_id={"space": 2 * other + core}, device_id_type=MESH
            )
        expected = expected + (1 + n_snap - 1 + n_space // 2 - 1)

    for halo in halos:
        halo.clear_missing()
    loads[0].wait()
    of_field.pack()
    pl.semaphore_wait(barrier, expected)
    of_field.start()
    loads[1].wait()
    loads[2].wait()

    mask_bits = mask[...].astype(F32).astype(BF16)

    def prepare(i, carry):
        here = rows_of(i, BLOCK)
        r, y = grid2(BLOCK, TALL)
        lines_of = mm(onehot((r >> 5) + i * (BLOCK // WIDE) == y), mask_bits)
        r, x = grid2(BLOCK, WIDE)
        one = jnp.where((r & (WIDE - 1)) == x, lines_of, 0.0).astype(BF16)
        m = mm(one, jnp.ones((WIDE, 128), BF16))
        mfull[here, :] = m
        for half in range(channels // 128):
            lanes = pl.ds(half * 128, 128)
            mixed_grad[here, lanes] = (
                cot[here, lanes].astype(F32) * m
            ).astype(BF16)
        return carry

    lax.fori_loop(0, BLOCKS, prepare, 0)
    of_mixed.pack()
    of_mixed.start()
    of_field.interior(f3)
    for n in (3, 4, 5, 6):
        loads[n].wait()
    for a in range(3):
        for b in range(3):
            w2t[a, pl.ds(b * channels, channels), :] = w2[
                2 - a, pl.ds((2 - b) * hidden_channels, hidden_channels), :
            ].T
            w1t[a, pl.ds(b * hidden_channels, hidden_channels), :] = w1[
                2 - a, pl.ds((2 - b) * channels, channels), :
            ].T
    pad = jnp.zeros((BAND, hidden_channels), BF16)
    for buf in (hall, pall):
        for a in range(3):
            for b in range(3):
                if a != b:
                    where = BAND * b if b < a else CELLS + BAND * (b - 1)
                    buf[pl.ds(where, BAND), pl.ds(a * hidden_channels, hidden_channels)] = pad
    of_mixed.interior(g3)
    of_field.wait_recv()
    of_field.borders(f3)

    def hidden_part(i, carry):
        here = rows_of(i, STEP)
        pre = jnp.zeros((STEP, hidden_channels), F32)
        for a in range(3):
            pre += mm(f3[rows_of(i, STEP, BAND * a), :], w1[a])
        pre = pre + b1[...]
        m = mfull[here, :]
        bell = 0.5 * (1.0 + lax.erf(pre * ROOT_HALF))
        hidden = (m * (pre * bell)).astype(BF16)
        mslope[here, :] = m * (bell + pre * jnp.exp(-0.5 * pre * pre) * INV_ROOT_TWO_PI)
        hidden_ref[here, :] = hidden
        for a in range(3):
            hall[rows_of(i, STEP, BAND * a), pl.ds(a * hidden_channels, hidden_channels)] = hidden
        return carry

    lax.fori_loop(0, CELLS // STEP, hidden_part, 0)
    of_hidden.pack()
    of_hidden.start()
    of_mixed.wait_recv()
    of_mixed.borders(g3)

    def pre_grad_part(i, carry):
        here = rows_of(i, STEP)
        g_hidden = jnp.zeros((STEP, hidden_channels), F32)
        for a in range(3):
            g_hidden += mm(g3[rows_of(i, STEP, BAND * a), :], w2t[a])
        g_pre = (g_hidden * mslope[here, :]).astype(BF16)
        pre_grad[here, :] = g_pre
        for a in range(3):
            pall[rows_of(i, STEP, BAND * a), pl.ds(a * hidden_channels, hidden_channels)] = g_pre
        return carry

    ones = jnp.ones((PART, CELLS), BF16)
    if fused:
        shard_c, shard_h = channels // n_space, hidden_channels // n_space
        share0, share1 = reductions[0].share, reductions[1].share
        quarter = share0.shape[3]

        def put(share, s, row, value):
            done = 0
            count = value.shape[0]
            while done < count:
                at = row + done
                k, within = at // quarter, at % quarter
                size = min(count - done, quarter - within)
                share[s % 2, s // 2, k, pl.ds(within, size), :] = value[done : done + size]
                done += size

        halves = channels // 128
        rows2 = 9 * shard_h * halves
        all_sums = mm(hall[...], g3[...], TN).astype(BF16)
        for b in range(3):
            sums = all_sums[:, (2 - b) * channels : (3 - b) * channels]
            for a in range(3):
                part = sums[(2 - a) * hidden_channels : (3 - a) * hidden_channels]
                t = 3 * a + b
                for s in range(n_space):
                    for half in range(halves):
                        put(
                            share0,
                            s,
                            (t * halves + half) * shard_h,
                            part[s * shard_h : (s + 1) * shard_h, half * 128 : half * 128 + 128],
                        )
        for s in range(n_space):
            left = n_snap * quarter - rows2
            if left:
                put(share0, s, rows2, jnp.zeros((left, 128), BF16))
        reductions[0].start_a()

        lax.fori_loop(0, CELLS // STEP, pre_grad_part, 0)
        of_pre.pack()
        of_pre.start()
        reductions[0].start_b()

        rows1 = 9 * shard_c
        r, _ = grid2(PART, 128)
        sum_pre = mm(ones, pre_grad[...])
        sum_mixed = mm(ones, mixed_grad[...])
        biases = jnp.where(
            r == 0,
            sum_pre,
            jnp.where(r == 1, sum_mixed[:, :128], jnp.where(r == 2, sum_mixed[:, 128:], 0.0)),
        ).astype(BF16)
        for s in range(n_space):
            put(share1, s, rows1, biases)
            left = n_snap * quarter - rows1 - PART
            if left:
                put(share1, s, rows1 + PART, jnp.zeros((left, 128), BF16))
        all_sums = mm(pall[...], f3[...], TN)
        for b in range(3):
            sums = all_sums[:, b * channels : (b + 1) * channels]
            for a in range(3):
                part = sums[a * hidden_channels : (a + 1) * hidden_channels].astype(BF16).T
                t = 3 * a + b
                for s in range(n_space):
                    put(share1, s, t * shard_c, part[s * shard_c : (s + 1) * shard_c])
        reductions[1].start_a()
    else:
        lax.fori_loop(0, CELLS // STEP, pre_grad_part, 0)
        of_pre.pack()
        of_pre.start()
        sum_pre = mm(ones, pre_grad[...])
        sum_mixed = mm(ones, mixed_grad[...])
        for b in range(3):
            sums = mm(hall[...], g3[:, pl.ds((2 - b) * channels, channels)], TN)
            for a in range(3):
                gw2[3 * a + b] = sums[(2 - a) * hidden_channels : (3 - a) * hidden_channels]
            sums = mm(pall[...], f3[:, pl.ds(b * channels, channels)], TN)
            for a in range(3):
                gw1[3 * a + b] = sums[a * hidden_channels : (a + 1) * hidden_channels].T
        gb1[...] = sum_pre[0:1]
        gb2[...] = sum_mixed[0:1]

    of_hidden.interior(h3)
    of_pre.interior(p3)
    if fused:
        reductions[1].start_b()
    of_hidden.wait_recv()
    of_hidden.borders(h3)

    def out_part(i, carry):
        here = rows_of(i, STEP)
        mixed = jnp.zeros((STEP, channels), F32)
        for a in range(3):
            mixed += mm(h3[rows_of(i, STEP, BAND * a), :], w2[a])
        mixed = mixed + b2[...]
        m = mfull[here, :]
        for half in range(channels // 128):
            lanes = pl.ds(half * 128, 128)
            field_out[here, lanes] = (
                field[here, lanes].astype(F32) + m * mixed[:, half * 128 : half * 128 + 128]
            ).astype(BF16)
        return carry

    def grad_part(i, carry):
        here = rows_of(i, STEP)
        total = jnp.zeros((STEP, channels), F32)
        for a in range(3):
            total += mm(p3[rows_of(i, STEP, BAND * a), :], w1t[a])
        grad_field[here, :] = (cot[here, :].astype(F32) + total).astype(BF16)
        return carry

    lax.fori_loop(0, CELLS // STEP, out_part, 0)
    stores[0].start()
    if fused:
        reductions[0].start_c()
    of_pre.wait_recv()
    of_pre.borders(p3)
    lax.fori_loop(0, CELLS // STEP, grad_part, 0)
    stores[1].start()
    if fused:
        reductions[0].start_d()
        reductions[1].start_c()
        reductions[0].finish(scale, whole)

        def get(row, count):
            pieces = []
            done = 0
            while done < count:
                at = row + done
                k, within = at // quarter, at % quarter
                size = min(count - done, quarter - within)
                pieces.append(whole[k, pl.ds(within, size), :])
                done += size
            return pieces[0] if len(pieces) == 1 else jnp.concatenate(pieces, axis=0)

        for t in range(9):
            for half in range(halves):
                gw2[t, :, pl.ds(half * 128, 128)] = get((t * halves + half) * shard_h, shard_h)
        reductions[1].start_d()
        reductions[1].finish(scale, whole)
        tail = get(rows1, PART)
        r, c = grid2(128, shard_h)
        pick = jnp.where(r == c + me * shard_h, 1.0, 0.0)
        gb1[...] = jnp.dot(
            tail, pick, preferred_element_type=F32, precision=lax.Precision.HIGHEST
        )[0:1]
        picked = jnp.zeros((PART, shard_c), F32)
        for half in range(halves):
            r, c = grid2(128, shard_c)
            pick = jnp.where(r + half * 128 == c + me * shard_c, 1.0, 0.0)
            picked = picked + jnp.where(
                lax.broadcasted_iota(jnp.int32, (PART, shard_c), 0) == 1 + half,
                jnp.dot(tail, pick, preferred_element_type=F32, precision=lax.Precision.HIGHEST),
                0.0,
            )
        gb2[...] = jnp.sum(picked, axis=0, keepdims=True)
        for t in range(9):
            gw1[t] = get(t * shard_c, shard_c)
        for red in reductions:
            red.wait_send()
    for halo in halos:
        halo.wait_send()
    for c in stores:
        c.wait()


def store_all(count, *refs):
    ins, outs, held, in_sem, out_sem = (
        refs[:count],
        refs[count : 2 * count],
        refs[2 * count : 3 * count],
        refs[-2],
        refs[-1],
    )
    pieces = []
    for n in range(count):
        rows = ins[n].shape[0]
        parts = 4 if rows % 64 == 0 else 1
        for k in range(parts):
            where = pl.ds(k * (rows // parts), rows // parts)
            i = len(pieces)
            pieces.append(
                (
                    pltpu.make_async_copy(ins[n].at[where], held[n].at[where], in_sem.at[i]),
                    pltpu.make_async_copy(held[n].at[where], outs[n].at[where], out_sem.at[i]),
                )
            )
    for load, _ in pieces:
        load.start()
    for load, store in pieces:
        load.wait()
        store.start()
    for _, store in pieces:
        store.wait()


def local(field_in, ocean_mask, cotangent, w_first, b_first, w_second, b_second):
    n_space, n_snap = lax.axis_size("space"), lax.axis_size("snap")
    tall, wide, channels = field_in.shape[2:]
    hidden_channels = w_first.shape[3]
    total = field_in.shape[0] * n_snap * n_space * tall * wide
    scale = 1.0 / math.sqrt(float(total))
    cells = tall * wide
    shard_c, shard_h = channels // n_space, hidden_channels // n_space
    fused = shard_c % 16 == 0 and shard_h % 16 == 0

    def halo_scratch(width):
        return [
            pltpu.VMEM((cells, width), BF16),
            pltpu.VMEM((2, EDGE, width), BF16),
            pltpu.VMEM((4, BAND, width), BF16),
            pltpu.VMEM((4, PART, width), BF16),
            pltpu.SemaphoreType.DMA((8,)),
            pltpu.SemaphoreType.DMA((8,)),
        ]

    widths = (channels, channels, hidden_channels, hidden_channels)
    scratch = []
    for width in widths:
        scratch += halo_scratch(width)
    scratch += [pltpu.VMEM((cells + 2 * BAND, 3 * width), BF16) for width in widths]
    scratch += [
        pltpu.VMEM((cells, 128), F32),
        pltpu.VMEM((cells, hidden_channels), F32),
        pltpu.VMEM((cells + 2 * BAND, 3 * hidden_channels), BF16),
        pltpu.VMEM((cells + 2 * BAND, 3 * hidden_channels), BF16),
        pltpu.VMEM((3, 3 * hidden_channels, channels), BF16),
        pltpu.VMEM((3, 3 * channels, hidden_channels), BF16),
        pltpu.VMEM((tall, wide), jnp.int32),
        pltpu.VMEM((cells, channels), BF16),
        pltpu.VMEM((3, 3 * channels, hidden_channels), BF16),
        pltpu.VMEM((1, hidden_channels), F32),
        pltpu.VMEM((3, 3 * hidden_channels, channels), BF16),
        pltpu.VMEM((1, channels), F32),
        pltpu.SemaphoreType.DMA((7,)),
        pltpu.VMEM((cells, channels), BF16),
        pltpu.VMEM((cells, channels), BF16),
        pltpu.SemaphoreType.DMA((2,)),
    ]
    if fused:
        chips = n_space // 2
        need = max(9 * shard_c * hidden_channels // 128 + PART, 9 * shard_h * channels // 128)
        quarter = -(-need // (PART * n_snap)) * PART
        for _ in range(2):
            piece = (quarter, 128)
            scratch += [
                pltpu.VMEM((2, chips, n_snap) + piece, BF16),
                pltpu.VMEM((chips, n_snap) + piece, BF16),
                pltpu.VMEM((n_snap, chips) + piece, BF16),
                pltpu.VMEM((n_snap - 1, chips) + piece, BF16),
                pltpu.VMEM((chips,) + piece, BF16),
                pltpu.VMEM((chips - 1,) + piece, BF16),
                pltpu.VMEM(piece, BF16),
                pltpu.VMEM((n_snap - 1,) + piece, BF16),
                pltpu.SemaphoreType.DMA,
                pltpu.SemaphoreType.DMA,
                pltpu.SemaphoreType.DMA((n_snap - 1,)),
                pltpu.SemaphoreType.DMA((n_snap - 1,)),
                pltpu.SemaphoreType.DMA((chips - 1,)),
                pltpu.SemaphoreType.DMA((chips - 1,)),
                pltpu.SemaphoreType.DMA((n_snap - 1,)),
                pltpu.SemaphoreType.DMA((n_snap - 1,)),
            ]
        scratch += [pltpu.VMEM((n_snap, quarter, 128), F32)]
        grads = [
            jax.ShapeDtypeStruct((9, shard_c, hidden_channels), F32),
            jax.ShapeDtypeStruct((9, shard_h, channels), F32),
            jax.ShapeDtypeStruct((1, shard_h), F32),
            jax.ShapeDtypeStruct((1, shard_c), F32),
        ]
    else:
        grads = [
            jax.ShapeDtypeStruct((9, channels, hidden_channels), F32),
            jax.ShapeDtypeStruct((9, hidden_channels, channels), F32),
            jax.ShapeDtypeStruct((1, hidden_channels), F32),
            jax.ShapeDtypeStruct((1, channels), F32),
        ]
    vmem = pl.BlockSpec(memory_space=pltpu.VMEM)
    results = pl.pallas_call(
        functools.partial(kernel, n_space, n_snap, fused, scale),
        out_shape=[jax.ShapeDtypeStruct((cells, channels), BF16)] * 2 + grads,
        in_specs=[pl.BlockSpec(memory_space=pl.ANY)] * 7,
        out_specs=[pl.BlockSpec(memory_space=pl.ANY)] * 2 + [vmem] * 4,
        scratch_shapes=scratch,
        compiler_params=pltpu.CompilerParams(
            collective_id=0, has_side_effects=True, vmem_limit_bytes=60 * 1024 * 1024
        ),
    )(
        field_in.reshape(cells, channels),
        ocean_mask.reshape(tall, wide),
        cotangent.reshape(cells, channels),
        w_first.reshape(3, 3 * channels, hidden_channels),
        b_first.reshape(1, hidden_channels),
        w_second.reshape(3, 3 * hidden_channels, channels),
        b_second.reshape(1, channels),
    )
    field_out, grad_field, gw1, gw2, gb1, gb2 = pl.pallas_call(
        functools.partial(store_all, 6),
        out_shape=[jax.ShapeDtypeStruct(value.shape, value.dtype) for value in results],
        in_specs=[pl.BlockSpec(memory_space=pl.ANY)] * 6,
        out_specs=[pl.BlockSpec(memory_space=pl.ANY)] * 6,
        scratch_shapes=[pltpu.VMEM(value.shape, value.dtype) for value in results]
        + [pltpu.SemaphoreType.DMA((12,)), pltpu.SemaphoreType.DMA((12,))],
        compiler_params=pltpu.CompilerParams(vmem_limit_bytes=60 * 1024 * 1024),
    )(*results)
    whole_shape = field_in.shape
    if not fused:
        sums = (
            lax.psum_scatter(gw1, "space", scatter_dimension=1, tiled=True),
            lax.psum_scatter(gw2, "space", scatter_dimension=1, tiled=True),
            lax.psum_scatter(gb1[0], "space", scatter_dimension=0, tiled=True),
            lax.psum_scatter(gb2[0], "space", scatter_dimension=0, tiled=True),
        )
        gw1, gw2, gb1, gb2 = [value * scale for value in lax.psum(sums, "snap")]
    return (
        field_out.reshape(whole_shape),
        grad_field.reshape(whole_shape),
        gw1.reshape(3, 3, shard_c, hidden_channels),
        gw2.reshape(3, 3, shard_h, channels),
        gb1.reshape(shard_h),
        gb2.reshape(shard_c),
    )


def solution(mesh):
    placed = (
        P("snap", "space", None, None, None),
        P("space", None, None),
        P("snap", "space", None, None, None),
        P(),
        P(),
        P(),
        P(),
    )
    return jax.shard_map(
        local,
        mesh=mesh,
        in_specs=placed,
        out_specs=(
            P("snap", "space", None, None, None),
            P("snap", "space", None, None, None),
            P(None, None, "space", None),
            P(None, None, "space", None),
            P("space"),
            P("space"),
        ),
        check_vma=False,
    )
```
